128 devices in a mesh: section: 2 (over x_hi), dp: 32 (over z, y, core), tensor: 2 (over x_lo).
Axes of the slice: x: 4 (x_hi: 2, x_lo: 2; x = x_hi * 2 + x_lo), y: 4, z: 4, core: 2. Of those that a mesh axis runs over, the one named last changes fastest.
Arguments:
- layer_input: bfloat16 [64, 128, 1024], P('dp', 'tensor'), may hold values from -6 to 6
- lengths: int32 [64, 4], P('dp'), may hold values from 1 to 96, 128 in all within a row
- cotangent: bfloat16 [64, 128, 1024], P('dp', 'tensor'), may hold values from -6 to 6
- norm1_gain: bfloat16 [2, 1024], P('section'), may hold values from 0.5 to 1.5
- norm1_shift: bfloat16 [2, 1024], P('section'), may hold values from -1.5 to 1.5
- qkv_weight: bfloat16 [2, 1024, 3, 1024], P('section', 'dp', None, 'tensor'), may hold values from -0.1875 to 0.1875
- qkv_bias: bfloat16 [2, 3, 1024], P('section', None, 'tensor'), may hold values from -1 to 1
- dense_weight: bfloat16 [2, 1024, 1024], P('section', 'dp', 'tensor'), may hold values from -0.5 to 0.5
- dense_bias: bfloat16 [2, 1024], P('section'), may hold values from -1 to 1
- norm2_gain: bfloat16 [2, 1024], P('section'), may hold values from 0.5 to 1.5
- norm2_shift: bfloat16 [2, 1024], P('section'), may hold values from -1.5 to 1.5
- up_weight: bfloat16 [2, 1024, 4096], P('section', 'dp', 'tensor'), may hold values from -0.1875 to 0.1875
- up_bias: bfloat16 [2, 4096], P('section', 'tensor'), may hold values from -1 to 1
- down_weight: bfloat16 [2, 1024, 4096], P('section', 'dp', 'tensor'), may hold values from -0.09375 to 0.09375
- down_bias: bfloat16 [2, 1024], P('section'), may hold values from -1 to 1
Outputs:
- layer_out: bfloat16 [2, 64, 128, 1024], P('section', 'dp', 'tensor')
- input_grad: bfloat16 [2, 64, 128, 1024], P('section', 'dp', 'tensor')
- grad_norm1_gain: float32 [2, 1024], P('section')
- grad_norm1_shift: float32 [2, 1024], P('section')
- grad_qkv_weight: float32 [2, 1024, 3, 1024], P('section', 'dp', None, 'tensor')
- grad_qkv_bias: float32 [2, 3, 1024], P('section', None, 'tensor')
- grad_dense_weight: float32 [2, 1024, 1024], P('section', 'dp', 'tensor')
- grad_dense_bias: float32 [2, 1024], P('section')
- grad_norm2_gain: float32 [2, 1024], P('section')
- grad_norm2_shift: float32 [2, 1024], P('section')
- grad_up_weight: float32 [2, 1024, 4096], P('section', 'dp', 'tensor')
- grad_up_bias: float32 [2, 4096], P('section', 'tensor')
- grad_down_weight: float32 [2, 1024, 4096], P('section', 'dp', 'tensor')
- grad_down_bias: float32 [2, 1024], P('section')
The draws below stay inside these ranges and needn't reach their ends.
Inputs may be any that keep to these rules, and one draw needn't show every extreme that they name: Each sequence's 4 lengths add up to 128; the longest is exactly 96.
All inputs are finite; a program needn't handle non-finite values.
Results may differ from the reference program's by a relative error of at most 0.025.
Values may be sent and summed in bfloat16 or wider, within the bound.
A program may use at most 128 MiB of HBM per device.

```python
import math
import jax
import jax.numpy as jnp
import numpy as np
from jax import lax

D = 1024
HEADS = 16
HEAD_DIM = 64
FF = 4096
ROWS = 128
DOCS = 4
SECTIONS = 2
BATCH = 64


def block_scale(own_key, extent, cuts, low, high):
    level = 1.0
    for position, shards_of in cuts:
        steps = jax.random.uniform(jax.random.fold_in(jax.random.fold_in(own_key, 6), position), (shards_of,), jnp.float32, low / len(cuts), high / len(cuts))
        level = level * jnp.repeat(jnp.exp(steps), extent[position] // shards_of).reshape((-1,) + (1,) * (len(extent) - 1 - position))
    return level


def split_up(amount, total, limit, skew):
    portions = [(1 << 20) // math.isqrt(rank ** skew) + 1 for rank in range(2, amount + 1)]
    rest, given = total - limit - (amount - 1), [1] * (amount - 1)
    while rest > 0:
        free = [i for i in range(amount - 1) if given[i] < limit]
        mass, remaining = sum([portions[i] for i in free]), rest
        for i in free:
            extra = min(limit - given[i], max(1, remaining * portions[i] // mass), rest)
            given[i] = given[i] + extra
            rest = rest - extra
    return np.array([limit] + given)


def ragged_sizes(own_key, number_of, total, reach, slope):
    if number_of == 2:
        one = jax.random.randint(own_key, (), max(1, total - reach), min(reach, total - 1) + 1)
        return jnp.stack([one, total - one])
    sizes = jnp.asarray(split_up(number_of, total, reach, slope), jnp.int32)
    couples = (number_of - 1) // 2
    donor, receiver = sizes[1:1 + 2 * couples:2], sizes[2:2 + 2 * couples:2]
    room = jnp.minimum(donor - 1, reach - receiver)
    moved = jax.random.randint(jax.random.fold_in(own_key, 1), (couples,), 0, 1 << 20) % (room + 1)
    sizes = sizes.at[1:1 + 2 * couples:2].set(donor - moved).at[2:2 + 2 * couples:2].set(receiver + moved)
    return sizes[jax.random.permutation(jax.random.fold_in(own_key, 2), number_of)]


def normal_values(key, shape, spread, most, shards=(), held_as=jnp.bfloat16):
    result = spread * jax.random.normal(key, shape, jnp.float32)
    if shards:
        result = result * block_scale(key, shape, shards, -0.22, 0.18)
    return jnp.clip(result, -most, most).astype(held_as)


def setup_inputs(seed: int = 0) -> dict:
    key_of = jax.random.split(jax.random.key(seed), 16)
    layer_input = normal_values(key_of[0], (BATCH, ROWS, D), 1.0, 6.0, ((0, 32), (1, 2)))
    lengths = jax.vmap(lambda own: ragged_sizes(own, DOCS, ROWS, ROWS // 2 + ROWS // 4, 2))(jax.random.split(key_of[1], BATCH)).reshape((BATCH, DOCS)).astype(jnp.int32)
    cotangent = normal_values(key_of[2], (BATCH, ROWS, D), 1.0, 6.0, ((0, 32), (1, 2)))
    norm1_gain = jnp.clip(1.0 + 0.1 * jax.random.normal(key_of[3], (SECTIONS, D), jnp.float32), 0.5, 1.5).astype(jnp.bfloat16)
    norm1_shift = normal_values(key_of[4], (SECTIONS, D), 0.3, 1.5, ((0, 2),))
    qkv_weight = normal_values(key_of[5], (SECTIONS, D, 3, D), D ** -0.5, 0.1875, ((0, 2), (1, 32), (3, 2)))
    qkv_bias = normal_values(key_of[6], (SECTIONS, 3, D), 0.2, 1.0, ((0, 2), (2, 2)))
    dense_weight = normal_values(key_of[7], (SECTIONS, D, D), (D // 8) ** -0.5, 0.5, ((0, 2), (1, 32), (2, 2)))
    dense_bias = normal_values(key_of[8], (SECTIONS, D), 0.2, 1.0, ((0, 2),))
    norm2_gain = jnp.clip(1.0 + 0.1 * jax.random.normal(key_of[9], (SECTIONS, D), jnp.float32), 0.5, 1.5).astype(jnp.bfloat16)
    norm2_shift = normal_values(key_of[10], (SECTIONS, D), 0.3, 1.5, ((0, 2),))
    up_weight = normal_values(key_of[11], (SECTIONS, D, FF), D ** -0.5, 0.1875, ((0, 2), (1, 32), (2, 2)))
    up_bias = normal_values(key_of[12], (SECTIONS, FF), 0.2, 1.0, ((0, 2), (1, 2)))
    down_weight = normal_values(key_of[13], (SECTIONS, D, FF), FF ** -0.5, 0.09375, ((0, 2), (1, 32), (2, 2)))
    down_bias = normal_values(key_of[14], (SECTIONS, D), 0.2, 1.0, ((0, 2),))
    return {"layer_input": layer_input, "lengths": lengths, "cotangent": cotangent, "norm1_gain": norm1_gain, "norm1_shift": norm1_shift, "qkv_weight": qkv_weight, "qkv_bias": qkv_bias, "dense_weight": dense_weight, "dense_bias": dense_bias, "norm2_gain": norm2_gain, "norm2_shift": norm2_shift, "up_weight": up_weight, "up_bias": up_bias, "down_weight": down_weight, "down_bias": down_bias}


EPSILON = 1e-05
HIGHEST = lax.Precision.HIGHEST

@jax.custom_vjp
def low(v):
    return lax.optimization_barrier(v.astype(jnp.bfloat16)).astype(jnp.float32)

@jax.custom_vjp
def low_back(v):
    return v

def low_keep(v):
    return (low(v), None)

def low_pass(kept, grad):
    return (grad,)

def back_keep(v):
    return (v, None)

def back_low(kept, grad):
    return (low(grad),)
low.defvjp(low_keep, low_pass)
low_back.defvjp(back_keep, back_low)

def layer_norm(values, gain, shift):
    centred = values - lax.optimization_barrier(jnp.mean(values, axis=-1, keepdims=True))
    inverse = lax.rsqrt(lax.optimization_barrier(jnp.mean(centred * centred, axis=-1, keepdims=True)) + EPSILON)
    return centred * inverse * gain + shift

def smooth_gate(values):
    return jax.nn.gelu(values, approximate=True)

def segment_ids(lengths, row_count):
    ends = jnp.cumsum(lengths, axis=-1).astype(jnp.int32)
    places = jnp.arange(row_count, dtype=jnp.int32)
    return lax.optimization_barrier(jnp.sum((places[:, None] >= ends[..., None, :]).astype(jnp.int32), axis=-1))

def attend_row(qkv_row, segments):
    row_count = qkv_row.shape[0]
    queries = qkv_row[:, 0].reshape(row_count, HEADS, HEAD_DIM)
    keys = qkv_row[:, 1].reshape(row_count, HEADS, HEAD_DIM)
    values = qkv_row[:, 2].reshape(row_count, HEADS, HEAD_DIM)
    places = jnp.arange(row_count, dtype=jnp.int32)
    slopes = jnp.exp2(-8.0 * jnp.arange(1, HEADS + 1).astype(jnp.float32) / HEADS)
    distance = (places[:, None] - places[None, :]).astype(jnp.float32)
    allowed = (segments[:, None] == segments[None, :]) & (places[None, :] <= places[:, None])
    scores = jnp.einsum('qhd,khd->hqk', queries, keys, precision=HIGHEST) * HEAD_DIM ** (-0.5) - slopes[:, None, None] * distance[None]
    scores = low_back(scores)
    scores = jnp.where(allowed[None], scores, -1e+30)
    highest = lax.optimization_barrier(jnp.max(scores, axis=-1, keepdims=True))
    exponent = jnp.exp(scores - highest)
    chances = low(exponent / lax.optimization_barrier(jnp.sum(exponent, axis=-1, keepdims=True)))
    mixed = jnp.einsum('hqk,khd->qhd', chances, values, precision=HIGHEST)
    return mixed.reshape(row_count, HEADS * HEAD_DIM)

def layer(current, params, segments):
    gain_one, shift_one, w_qkv, qkv_bias, w_dense, dense_bias, gain_two, shift_two, w_up, up_bias, w_down, down_bias = params
    normed = low(layer_norm(current, gain_one, shift_one))
    projected = jnp.einsum('brd,dcf->brcf', normed, w_qkv, precision=HIGHEST) + qkv_bias
    projected = low_back(low(projected))
    attend_saved = jax.checkpoint(attend_row)
    mixed = lax.map(lambda pair: attend_saved(pair[0], pair[1]), (projected, segments))
    mixed = low_back(low(mixed))
    attended = jnp.einsum('brf,df->brd', mixed, w_dense, precision=HIGHEST)
    hidden = current + dense_bias + low_back(attended)
    normed_two = low(layer_norm(hidden, gain_two, shift_two))
    raised = low_back(jnp.einsum('brd,df->brf', normed_two, w_up, precision=HIGHEST) + up_bias)
    activated = low(smooth_gate(raised))
    lowered = jnp.einsum('brf,df->brd', activated, w_down, precision=HIGHEST)
    return hidden + down_bias + low_back(lowered)

def reference(layer_input, lengths, cotangent, norm1_gain, norm1_shift, qkv_weight, qkv_bias, dense_weight, dense_bias, norm2_gain, norm2_shift, up_weight, up_bias, down_weight, down_bias):
    segments = segment_ids(lengths, ROWS)
    params = tuple((member.astype(jnp.float32) for member in (norm1_gain, norm1_shift, qkv_weight, qkv_bias, dense_weight, dense_bias, norm2_gain, norm2_shift, up_weight, up_bias, down_weight, down_bias)))
    first_input = layer_input.astype(jnp.float32)

    def whole(start_input, all_params, injected):
        first_params = tuple((member[0] for member in all_params))
        second_params = tuple((member[1] for member in all_params))
        first_out = layer(start_input, first_params, segments)
        second_input = low_back(low(first_out)) + injected
        second_out = layer(second_input, second_params, segments)
        return (first_out, second_out)
    (first_out, second_out), pull = jax.vjp(whole, first_input, params, jnp.zeros_like(first_input))
    first_grad, param_grads, second_grad = pull((jnp.zeros_like(first_out), cotangent.astype(jnp.float32)))
    layer_out = jnp.stack([first_out, second_out]).astype(jnp.bfloat16)
    input_grad = jnp.stack([first_grad, second_grad]).astype(jnp.bfloat16)
    return (layer_out, input_grad, param_grads[0], param_grads[1], param_grads[2], param_grads[3], param_grads[4], param_grads[5], param_grads[6], param_grads[7], param_grads[8], param_grads[9], param_grads[10], param_grads[11])
```

```python
import jax
import jax.numpy as jnp
from jax import lax
from jax.experimental import pallas as pl
from jax.experimental.pallas import tpu as pltpu
from jax.sharding import PartitionSpec as P

D = 1024
HEADS = 16
HEAD_DIM = 64
FF = 4096
ROWS = 128
EPSILON = 1e-05
GELU_A = 0.79788456
GELU_B = 0.044715

SEQS = 2
HALF = 64
HEADS_HERE = HEADS // 2
WIDTH = HEADS_HERE * HEAD_DIM
HIDDEN = FF // 2
QKV_AT = 0
DENSE_AT = 3 * WIDTH
UP_AT = DENSE_AT + WIDTH
DOWN_AT = UP_AT + HIDDEN
COLUMNS = DOWN_AT + HIDDEN
TILE = 512

BF = jnp.bfloat16
F32 = jnp.float32
MESH = pl.DeviceIdType.MESH

NN = (((1,), (0,)), ((), ()))
NT = (((1,), (1,)), ((), ()))
TN = (((0,), (0,)), ((), ()))


def mm(left, right, dims=NN):
    return lax.dot_general(left, right, dims, preferred_element_type=F32)


class Links:
    def __init__(self, send_sems, recv_sems):
        self.send_sems = send_sems
        self.recv_sems = recv_sems
        self.names = {}
        self.started = []

    def index(self, name):
        return self.names.setdefault(name, len(self.names))

    def copy(self, name, src, dst, device):
        i = self.index(name)
        return pltpu.make_async_remote_copy(
            src_ref=src,
            dst_ref=dst,
            send_sem=self.send_sems.at[i],
            recv_sem=self.recv_sems.at[i],
            device_id=device,
            device_id_type=MESH,
        )

    def send(self, name, src, dst, device):
        copy = self.copy(name, src, dst, device)
        copy.start()
        self.started.append(copy)

    def arrived(self, name, landing, device):
        self.copy(name, landing, landing, device).wait_recv()

    def drain(self):
        for copy in self.started:
            copy.wait_send()
        self.started = []


def four(value):
    return lax.rem(value + 8, 4)


class Place:
    def __init__(self):
        self.section = lax.axis_index("section")
        self.tensor = lax.axis_index("tensor")
        dp = lax.axis_index("dp")
        self.core = lax.rem(dp, 2)
        self.y = lax.rem(lax.div(dp, 2), 4)
        self.z = lax.div(dp, 8)
        self.d = 1 - 2 * self.core

    def dp(self, z, y, core):
        return {"dp": (z * 4 + y) * 2 + core}

    def along(self, axis, offset):
        if axis == "y":
            return self.dp(self.z, four(self.y + offset), self.core)
        return self.dp(four(self.z + offset), self.y, self.core)

    def sibling(self):
        return self.dp(self.z, self.y, 1 - self.core)

    def peer(self):
        return {"tensor": 1 - self.tensor}

    def other_section(self):
        return {"section": 1 - self.section}


FIRST = ("y", "z")
SECOND = ("z", "y")


def gather_weights(place, links, w):
    z, y, core, d = place.z, place.y, place.core, place.d

    def piece(half, first, second):
        if half == 0:
            return w.at[four(z + second), four(y + first), core, 0]
        return w.at[four(z + first), four(y + second), core, 1]

    def send(name, half, spot, axis, offset):
        ref = piece(half, *spot)
        links.send(("ag", name, half), ref, ref, place.along(axis, offset))

    def arrived(name, half, spot):
        links.arrived(("ag", name, half), piece(half, *spot), place.sibling())

    def second_sends(half, k, first):
        send(("s+", k), half, (first, 0), SECOND[half], d)
        send(("s-", k), half, (first, 0), SECOND[half], -d)

    firsts = (0, -d, d, 2)
    for half in range(2):
        send("f+", half, (0, 0), FIRST[half], d)
        send("f-", half, (0, 0), FIRST[half], -d)
    for half in range(2):
        second_sends(half, 0, 0)
    for half in range(2):
        arrived("f+", half, (-d, 0))
        send("fr", half, (-d, 0), FIRST[half], d)
        second_sends(half, 1, -d)
    for half in range(2):
        arrived("f-", half, (d, 0))
        second_sends(half, 2, d)
    for half in range(2):
        arrived(("s+", 0), half, (0, -d))
        send(("sr", 0), half, (0, -d), SECOND[half], d)
    for half in range(2):
        arrived("fr", half, (2, 0))
        second_sends(half, 3, 2)

    def group(half, second, of_core):
        if half == 0:
            return w.at[four(z + second), :, of_core, 0]
        return w.at[:, four(y + second), of_core, 1]

    def to_sibling(half, j, second):
        ref = group(half, second, core)
        links.send(("ag", "sib", j, half), ref, ref, place.sibling())

    for half in range(2):
        to_sibling(half, 0, 0)
    for k in range(1, 4):
        for half in range(2):
            arrived(("s+", k), half, (firsts[k], -d))
            send(("sr", k), half, (firsts[k], -d), SECOND[half], d)
    for half in range(2):
        to_sibling(half, 1, -d)
    for k in range(4):
        for half in range(2):
            arrived(("s-", k), half, (firsts[k], d))
    for half in range(2):
        to_sibling(half, 2, d)
    for k in range(4):
        for half in range(2):
            arrived(("sr", k), half, (firsts[k], 2))
    for half in range(2):
        to_sibling(half, 3, 2)
    for j, second in enumerate((0, d, -d, 2)):
        for half in range(2):
            links.arrived(
                ("ag", "sib", j, half), group(half, second, 1 - core), place.sibling()
            )


def add_rows(target, parts):
    def one(j, carry):
        for at in range(0, COLUMNS, 2048):
            cols = pl.ds(at, 2048)
            total = parts[0](j, cols).astype(F32)
            for part in parts[1:]:
                total = total + part(j, cols).astype(F32)
            target(j, cols, total)
        return carry

    lax.fori_loop(0, 4, one, 0)


def scatter_grads(place, links, g, sb, r1, r2, r3, q, outs, small, small_in, small_outs):
    z, y, core, d = place.z, place.y, place.core, place.d
    axes = ("z", "y")
    other_axes = ("y", "z")

    def group(half, offset, of_core):
        if half == 0:
            return g.at[four(z + offset), :, of_core, 0]
        return g.at[:, four(y + offset), of_core, 1]

    def own_part(half, offset):
        def load(j, cols):
            if half == 0:
                return g[four(z + offset), j, core, 0, :, cols]
            return g[j, four(y + offset), core, 1, :, cols]

        return load

    def of(ref, *lead):
        return lambda j, cols: ref[(*lead, j, slice(None), cols)]

    def into(ref, *lead):
        def store(j, cols, value):
            ref[(*lead, j, slice(None), cols)] = value.astype(BF)

        return store

    mine = (0, d, -d, 2)
    theirs = (0, -d, d, 2)
    for slot in (3, 2, 1, 0):
        for half in range(2):
            links.send(
                ("rs", "sib", slot, half),
                group(half, theirs[slot], 1 - core),
                sb.at[half, slot],
                place.sibling(),
            )

    partners = (
        place.peer(),
        place.sibling(),
        place.dp(z, y + 1 - 2 * lax.rem(y, 2), core),
        place.dp(z, 3 - y, core),
        place.dp(z + 1 - 2 * lax.rem(z, 2), y, core),
        place.dp(3 - z, y, core),
    )

    def small_start(step):
        rows = pl.ds(0, 8 if step == 0 else 16)
        links.send(
            ("small", step), small.at[step, rows], small_in.at[step, rows], partners[step]
        )

    def small_end(step):
        rows = pl.ds(0, 8 if step == 0 else 16)
        links.arrived(("small", step), small_in.at[step, rows], partners[step])
        if step == 0:
            small[1, 0:8] = small[0, 0:8] + small_in[0, 0:8]
            small[1, 8:16] = small[0, 8:16]
        else:
            small[step + 1] = small[step] + small_in[step]

    def from_sibling(slot, half):
        links.arrived(("rs", "sib", slot, half), sb.at[half, slot], place.sibling())

    small_start(0)
    for half in range(2):
        from_sibling(3, half)
        add_rows(into(sb, half, 3), [of(sb, half, 3), own_part(half, mine[3])])
        links.send(("rs", "r1", half), sb.at[half, 3], r1.at[half], place.along(axes[half], d))
    small_end(0)
    small_start(1)
    for half in range(2):
        from_sibling(2, half)
        add_rows(into(sb, half, 2), [of(sb, half, 2), own_part(half, mine[2])])
        links.send(("rs", "r3", half), sb.at[half, 2], r3.at[half], place.along(axes[half], -d))
    small_end(1)
    small_start(2)
    for half in range(2):
        from_sibling(1, half)
        links.arrived(("rs", "r1", half), r1.at[half], place.sibling())
        add_rows(
            into(sb, half, 1), [of(sb, half, 1), own_part(half, mine[1]), of(r1, half)]
        )
        links.send(("rs", "r2", half), sb.at[half, 1], r2.at[half], place.along(axes[half], d))
    small_end(2)
    small_start(3)
    for half in range(2):
        from_sibling(0, half)
        links.arrived(("rs", "r3", half), r3.at[half], place.sibling())
        add_rows(
            into(sb, half, 0), [of(sb, half, 0), own_part(half, mine[0]), of(r3, half)]
        )
    small_end(3)
    small_start(4)
    spots = (y, z)
    for half in range(2):
        links.arrived(("rs", "r2", half), r2.at[half], place.sibling())
        add_rows(into(sb, half, 0), [of(sb, half, 0), of(r2, half)])
        links.send(
            ("rs", "q0", half),
            sb.at[half, 0, four(spots[half] + 2)],
            q.at[half, 0],
            place.along(other_axes[half], d),
        )
        links.send(
            ("rs", "q2", half),
            sb.at[half, 0, four(spots[half] - d)],
            q.at[half, 2],
            place.along(other_axes[half], -d),
        )
    small_end(4)
    small_start(5)
    for half in range(2):
        links.arrived(("rs", "q0", half), q.at[half, 0], place.sibling())
        spot = four(spots[half] + d)
        for at in range(0, COLUMNS, 2048):
            cols = pl.ds(at, 2048)
            total = q[half, 0, :, cols].astype(F32) + sb[half, 0, spot, :, cols].astype(F32)
            q[half, 0, :, cols] = total.astype(BF)
        links.send(
            ("rs", "q1", half), q.at[half, 0], q.at[half, 1], place.along(other_axes[half], d)
        )
    small_end(5)
    ends = ((outs[0], QKV_AT), (outs[1], DENSE_AT), (outs[2], UP_AT), (outs[3], DOWN_AT))
    for half in range(2):
        links.arrived(("rs", "q2", half), q.at[half, 2], place.sibling())
        links.arrived(("rs", "q1", half), q.at[half, 1], place.sibling())
        for out, start in ends:
            for at in range(0, out.shape[1], TILE):
                cols = pl.ds(start + at, TILE)
                out[half * 16 : half * 16 + 16, at : at + TILE] = (
                    sb[half, 0, spots[half], :, cols].astype(F32)
                    + q[half, 1, :, cols].astype(F32)
                    + q[half, 2, :, cols].astype(F32)
                )
    n1g, n1s, qkvb, denseb, n2g, n2s, upb, downb = small_outs
    for row, out in enumerate((n1g, n1s, denseb, n2g, n2s, downb)):
        out[...] = small[6, row : row + 1]
    upb[:, 0:D] = small[6, 8:9]
    upb[:, D : 2 * D] = small[6, 9:10]
    qkvb[0, 0:1] = small[6, 10:11, 0:WIDTH]
    qkvb[0, 1:2] = small[6, 10:11, WIDTH : 2 * WIDTH]
    qkvb[0, 2:3] = small[6, 11:12, 0:WIDTH]


def normalise(values):
    mean = jnp.mean(values, axis=-1, keepdims=True)
    centred = values - mean
    inverse = lax.rsqrt(jnp.mean(centred * centred, axis=-1, keepdims=True) + EPSILON)
    return centred * inverse, inverse


def normalise_back(grad, normed, inverse, gain):
    scaled = grad * gain
    one = jnp.mean(scaled, axis=-1, keepdims=True)
    two = jnp.mean(scaled * normed, axis=-1, keepdims=True)
    return inverse * (scaled - one - normed * two)


def column_sum(values):
    return jnp.sum(values, axis=0, keepdims=True)


def both(ref, t, cols=slice(None)):
    return jnp.concatenate([ref[0, t, :, cols], ref[1, t, :, cols]], axis=0)


def put_both(ref, t, cols, value):
    ref[0, t, :, cols] = value[:HALF]
    ref[1, t, :, cols] = value[HALF:]


def whole_columns(w, cols):
    return w[:, :, :, :, :, cols].reshape(D, -1)


def weight_grad(g, left, right, start, count):
    def one(i, carry):
        at = pl.multiple_of(i * 256, 256)
        piece = left[:, :, :, pl.ds(at, 256)].reshape(SEQS * ROWS, 256)
        for col in range(0, count, TILE):
            size = min(TILE, count - col)
            part = right[:, :, :, col : col + size].reshape(SEQS * ROWS, size)
            value = mm(piece, part, TN).astype(BF)
            g[i, :, :, :, :, start + col : start + col + size] = value.reshape(4, 2, 2, 16, size)
        return carry

    lax.fori_loop(0, 4, one, 0)


def add_partial(w, start, count, load, store):
    rows = load()

    def one(i, carry):
        at = pl.multiple_of(i * 256, 256)
        piece = w[i, :, :, :, :, start : start + count].reshape(256, count)
        store(pl.ds(at, 256), mm(rows, piece, NT))
        return carry

    lax.fori_loop(0, 4, one, 0)


def score_bias(lengths, seq):
    queries = lax.broadcasted_iota(jnp.int32, (ROWS, ROWS), 0)
    keys = lax.broadcasted_iota(jnp.int32, (ROWS, ROWS), 1)
    query_segment = jnp.zeros((ROWS, ROWS), jnp.int32)
    key_segment = jnp.zeros((ROWS, ROWS), jnp.int32)
    end = 0
    for doc in range(4):
        end = end + lengths[seq, doc]
        query_segment = query_segment + (queries >= end).astype(jnp.int32)
        key_segment = key_segment + (keys >= end).astype(jnp.int32)
    allowed = (query_segment == key_segment) & (keys <= queries)
    return jnp.where(allowed, 0.0, -1e30), (queries - keys).astype(F32)


def halves_of_pair():
    lanes = lax.broadcasted_iota(jnp.int32, (1, 128), 1).astype(F32)
    low = jnp.where(lanes < HEAD_DIM, 1.0, 0.0).astype(BF)
    high = jnp.where(lanes < HEAD_DIM, 0.0, 1.0).astype(BF)
    return low, high


def main_kernel(
    x_ref, lengths, cot_ref, n1g, n1s, wqkv, qkvb, wdense, denseb, n2g, n2s, wup, upb, wdown, downb,
    y_out, gx_out, dn1g, dn1s, dqkv, dqkvb, ddense, ddenseb, dn2g, dn2s, dup, dupb, ddown, ddownb,
    w, g, sb, r1, r2, r3, q, small, small_in,
    xs, inbox, outbox, a_all, qkv, o_all, p_all, hidden, xh1, xh2, inv1, inv2, c_all, act, slope_u,
    gz_all, gu, gat_all, go, gqkv, part_out, part_in, wide, ghid, send_sems, recv_sems,
):
    place = Place()
    links = Links(send_sems, recv_sems)
    t, other = place.tensor, 1 - place.tensor

    barrier = pltpu.get_barrier_semaphore()
    neighbours = [
        place.along("y", 1),
        place.along("y", -1),
        place.along("z", 1),
        place.along("z", -1),
        place.sibling(),
        place.peer(),
        place.other_section(),
    ]
    for neighbour in neighbours:
        pl.semaphore_signal(barrier, inc=1, device_id=neighbour, device_id_type=MESH)
    for half in range(2):
        rows = slice(half * 16, half * 16 + 16)
        for ref, start in ((wqkv, QKV_AT), (wdense, DENSE_AT), (wup, UP_AT), (wdown, DOWN_AT)):
            w[place.z, place.y, place.core, half, :, start : start + ref.shape[1]] = ref[rows, :]
    pl.semaphore_wait(barrier, len(neighbours))

    gather_weights(place, links, w)

    @pl.when(place.section == 0)
    def _():
        xs[...] = x_ref[...]

    @pl.when(place.section == 1)
    def _():
        links.arrived("forward", inbox, place.other_section())
        xs[...] = inbox[...]

    def share(name, ref):
        links.send(name, ref.at[:, t], ref.at[:, t], place.peer())

    def shared(name, ref):
        links.arrived(name, ref.at[:, other], place.peer())

    gain1, shift1 = n1g[...].astype(F32), n1s[...].astype(F32)
    gain2, shift2 = n2g[...].astype(F32), n2s[...].astype(F32)

    for s in range(SEQS):
        normed, inverse = normalise(xs[s].astype(F32))
        xh1[s] = normed
        inv1[s] = jnp.broadcast_to(inverse, (HALF, 128))
        a_all[s, t] = (normed * gain1 + shift1).astype(BF)
    share("a", a_all)

    def project(half):
        rows = both(a_all, half)
        for kind in range(3):
            cols = slice(kind * WIDTH, (kind + 1) * WIDTH)
            value = mm(rows, whole_columns(w, cols)) + qkvb[0, kind : kind + 1].astype(F32)
            put_both(qkv, half, cols, value.astype(BF))

    project(t)
    shared("a", a_all)
    project(other)

    masks = halves_of_pair()
    tensor_scale = jnp.where(t == 0, 1.0, 2.0 ** (-8.0 * HEADS_HERE / HEADS))

    def attend(s, carry):
        bias, distance = score_bias(lengths, s)
        distance = distance * tensor_scale
        for pair in range(HEADS_HERE // 2):
            cols = slice(pair * 128, pair * 128 + 128)
            queries = qkv[s, :, :, cols].reshape(ROWS, 128)
            keys = qkv[s, :, :, WIDTH + pair * 128 : WIDTH + pair * 128 + 128].reshape(ROWS, 128)
            values = qkv[s, :, :, 2 * WIDTH + pair * 128 : 2 * WIDTH + pair * 128 + 128]
            values = values.reshape(ROWS, 128)
            mixed = None
            for side in range(2):
                head = pair * 2 + side
                slope = 2.0 ** (-8.0 * (head + 1) / HEADS)
                scores = mm(queries * masks[side], keys, NT) * HEAD_DIM ** (-0.5)
                scores = scores + (bias - slope * distance)
                exponent = jnp.exp(scores - jnp.max(scores, axis=-1, keepdims=True))
                chances = exponent / jnp.sum(exponent, axis=-1, keepdims=True)
                p_all[s, head] = chances
                term = mm(chances.astype(BF), values * masks[side])
                mixed = term if mixed is None else mixed + term
            o_all[s, :, :, cols] = mixed.astype(BF).reshape(2, HALF, 128)
        return carry

    lax.fori_loop(0, SEQS, attend, 0)

    def reduce_start(name, k, start, count, source):
        def to_peer(cols, value):
            part_out[k, 0, :, cols] = value[:HALF].astype(BF)
            part_out[k, 1, :, cols] = value[HALF:].astype(BF)

        add_partial(w, start, count, lambda: both(source, other), to_peer)
        links.send(name, part_out.at[k], part_in.at[k], place.peer())

        def keep(cols, value):
            wide[0, :, cols] = value[:HALF]
            wide[1, :, cols] = value[HALF:]

        add_partial(w, start, count, lambda: both(source, t), keep)

    def reduce_end(name, k):
        links.arrived(name, part_in.at[k], place.peer())

    reduce_start("attended", 0, DENSE_AT, WIDTH, o_all)
    reduce_end("attended", 0)
    for s in range(SEQS):
        value = xs[s].astype(F32) + denseb[...].astype(F32)
        value = value + (wide[s] + part_in[0, s].astype(F32))
        hidden[s] = value
        normed, inverse = normalise(value)
        xh2[s] = normed
        inv2[s] = jnp.broadcast_to(inverse, (HALF, 128))
        c_all[s, t] = (normed * gain2 + shift2).astype(BF)
    share("c", c_all)

    def raise_rows(half):
        rows = both(c_all, half)

        def one(i, carry):
            at = pl.multiple_of(i * TILE, TILE)
            u = mm(rows, whole_columns(w, pl.ds(UP_AT + at, TILE)))
            u = u + upb[:, pl.ds(at, TILE)].astype(F32)
            square = u * u
            tanh = jnp.tanh(GELU_A * u * (1.0 + GELU_B * square))
            inner = GELU_A * (1.0 + (3.0 * GELU_B) * square)
            put_both(act, half, pl.ds(at, TILE), (0.5 * u * (1.0 + tanh)).astype(BF))
            slope = 0.5 * (1.0 + tanh) + 0.5 * u * (1.0 - tanh * tanh) * inner
            put_both(slope_u, half, pl.ds(at, TILE), slope)
            return carry

        lax.fori_loop(0, HIDDEN // TILE, one, 0)

    raise_rows(t)
    shared("c", c_all)
    raise_rows(other)
    reduce_start("lowered", 1, DOWN_AT, HIDDEN, act)
    reduce_end("lowered", 1)
    for s in range(SEQS):
        value = hidden[s] + downb[...].astype(F32) + (wide[s] + part_in[1, s].astype(F32))
        outbox[0, s] = value.astype(BF)
        y_out[s] = value.astype(BF)

    @pl.when(place.section == 0)
    def _():
        links.copy("forward", outbox.at[0], inbox, place.other_section()).start()

    @pl.when(place.section == 0)
    def _():
        links.arrived("backward", inbox, place.other_section())
        xs[...] = inbox[...]

    @pl.when(place.section == 1)
    def _():
        xs[...] = cot_ref[...]

    for s in range(SEQS):
        gz_all[s, t] = xs[s]
    share("gz", gz_all)

    def lower_back(half):
        rows = both(gz_all, half)

        def one(i, carry):
            at = pl.multiple_of(i * TILE, TILE)
            value = mm(rows, whole_columns(w, pl.ds(DOWN_AT + at, TILE)))
            value = value * both(slope_u, half, pl.ds(at, TILE))
            put_both(gu, half, pl.ds(at, TILE), value.astype(BF))
            return carry

        lax.fori_loop(0, HIDDEN // TILE, one, 0)

    lower_back(t)
    shared("gz", gz_all)
    lower_back(other)
    reduce_start("gc", 2, UP_AT, HIDDEN, gu)
    weight_grad(g, gz_all, act, DOWN_AT, HIDDEN)
    reduce_end("gc", 2)
    sums = [0.0] * 6
    for s in range(SEQS):
        grad = wide[s] + part_in[2, s].astype(F32)
        normed = xh2[s]
        gy = xs[s].astype(F32)
        sums[3] = sums[3] + column_sum(grad * normed)
        sums[4] = sums[4] + column_sum(grad)
        sums[5] = sums[5] + column_sum(gy)
        value = gy + normalise_back(grad, normed, inv2[s][:, 0:1], gain2)
        ghid[s] = value
        sums[2] = sums[2] + column_sum(value)
        gat_all[s, t] = value.astype(BF)
    share("gat", gat_all)

    def dense_back(half):
        value = mm(both(gat_all, half), whole_columns(w, slice(DENSE_AT, DENSE_AT + WIDTH)))
        put_both(go, half, slice(None), value.astype(BF))

    dense_back(t)
    weight_grad(g, c_all, gu, UP_AT, HIDDEN)
    shared("gat", gat_all)
    dense_back(other)

    def attend_back(s, carry):
        for pair in range(HEADS_HERE // 2):
            cols = slice(pair * 128, pair * 128 + 128)
            queries = qkv[s, :, :, cols].reshape(ROWS, 128)
            keys = qkv[s, :, :, WIDTH + pair * 128 : WIDTH + pair * 128 + 128].reshape(ROWS, 128)
            values = qkv[s, :, :, 2 * WIDTH + pair * 128 : 2 * WIDTH + pair * 128 + 128]
            values = values.reshape(ROWS, 128)
            grads = go[s, :, :, cols].reshape(ROWS, 128)
            totals = [None, None, None]
            for side in range(2):
                chances = p_all[s, pair * 2 + side]
                out_grad = grads * masks[side]
                chance_grad = mm(out_grad, values, NT)
                inner = jnp.sum(chances * chance_grad, axis=-1, keepdims=True)
                score_grad = (chances * (chance_grad - inner)).astype(BF)
                terms = (
                    mm(score_grad, keys * masks[side]),
                    mm(score_grad, queries * masks[side], TN),
                    mm(chances.astype(BF), out_grad, TN),
                )
                totals = [b if a is None else a + b for a, b in zip(totals, terms)]
            scale = HEAD_DIM ** (-0.5)
            for kind, value in enumerate((totals[0] * scale, totals[1] * scale, totals[2])):
                at = kind * WIDTH + pair * 128
                gqkv[s, :, :, at : at + 128] = value.astype(BF).reshape(2, HALF, 128)
        return carry

    lax.fori_loop(0, SEQS, attend_back, 0)
    reduce_start("ga", 3, QKV_AT, 3 * WIDTH, gqkv)
    weight_grad(g, gat_all, o_all, DENSE_AT, WIDTH)
    reduce_end("ga", 3)
    for s in range(SEQS):
        grad = wide[s] + part_in[3, s].astype(F32)
        normed = xh1[s]
        sums[0] = sums[0] + column_sum(grad * normed)
        sums[1] = sums[1] + column_sum(grad)
        value = ghid[s] + normalise_back(grad, normed, inv1[s][:, 0:1], gain1)
        outbox[1, s] = value.astype(BF)
        gx_out[s] = value.astype(BF)

    @pl.when(place.section == 1)
    def _():
        links.copy("backward", outbox.at[1], inbox, place.other_section()).start()

    weight_grad(g, a_all, gqkv, QKV_AT, 3 * WIDTH)

    small[0, 6:8] = jnp.zeros((2, D), F32)
    small[0, 12:16] = jnp.zeros((4, D), F32)
    for row in range(6):
        small[0, row : row + 1] = sums[row]
    for i in range(2):
        piece = gu[:, :, :, i * D : (i + 1) * D].reshape(SEQS * ROWS, D).astype(F32)
        small[0, 8 + i : 9 + i] = column_sum(piece)
    piece = gqkv[:, :, :, 0:D].reshape(SEQS * ROWS, D).astype(F32)
    small[0, 10:11] = column_sum(piece)
    piece = gqkv[:, :, :, D : 3 * WIDTH].reshape(SEQS * ROWS, WIDTH).astype(F32)
    small[0, 11:12, 0:WIDTH] = column_sum(piece)
    small[0, 11:12, WIDTH:D] = jnp.zeros((1, D - WIDTH), F32)

    scatter_grads(
        place, links, g, sb, r1, r2, r3, q, (dqkv, ddense, dup, ddown), small, small_in,
        (dn1g, dn1s, dqkvb, ddenseb, dn2g, dn2s, dupb, ddownb),
    )
    links.drain()

    @pl.when(place.section == 0)
    def _():
        links.copy("forward", outbox.at[0], inbox, place.other_section()).wait_send()

    @pl.when(place.section == 1)
    def _():
        links.copy("backward", outbox.at[1], inbox, place.other_section()).wait_send()


def local(
    layer_input,
    lengths,
    cotangent,
    norm1_gain,
    norm1_shift,
    qkv_weight,
    qkv_bias,
    dense_weight,
    dense_bias,
    norm2_gain,
    norm2_shift,
    up_weight,
    up_bias,
    down_weight,
    down_bias,
):
    share = qkv_weight.shape[1]
    vmem = pl.BlockSpec(memory_space=pltpu.VMEM)
    smem = pl.BlockSpec(memory_space=pltpu.SMEM)
    shape = jax.ShapeDtypeStruct
    tokens = (SEQS, HALF, D)
    row = shape((1, D), F32)
    out_shape = (
        shape(tokens, BF),
        shape(tokens, BF),
        row,
        row,
        shape((share, 3 * WIDTH), F32),
        shape((1, 3, WIDTH), F32),
        shape((share, WIDTH), F32),
        row,
        row,
        row,
        shape((share, HIDDEN), F32),
        shape((1, HIDDEN), F32),
        shape((share, HIDDEN), F32),
        row,
    )
    block = (4, 4, 2, 2, 16, COLUMNS)

    def all_tokens(width, dtype):
        return pltpu.VMEM((SEQS, 2, HALF, width), dtype)

    scratch = [
        pltpu.VMEM(block, BF),
        pltpu.VMEM(block, BF),
        pltpu.VMEM((2, 4, 4, 16, COLUMNS), BF),
        pltpu.VMEM((2, 4, 16, COLUMNS), BF),
        pltpu.VMEM((2, 4, 16, COLUMNS), BF),
        pltpu.VMEM((2, 4, 16, COLUMNS), BF),
        pltpu.VMEM((2, 3, 16, COLUMNS), BF),
        pltpu.VMEM((7, 16, D), F32),
        pltpu.VMEM((6, 16, D), F32),
        pltpu.VMEM(tokens, BF),
        pltpu.VMEM(tokens, BF),
        pltpu.VMEM((2,) + tokens, BF),
        all_tokens(D, BF),
        all_tokens(3 * WIDTH, BF),
        all_tokens(WIDTH, BF),
        pltpu.VMEM((SEQS, HEADS_HERE, ROWS, ROWS), F32),
        pltpu.VMEM(tokens, F32),
        pltpu.VMEM(tokens, F32),
        pltpu.VMEM(tokens, F32),
        pltpu.VMEM((SEQS, HALF, 128), F32),
        pltpu.VMEM((SEQS, HALF, 128), F32),
        all_tokens(D, BF),
        all_tokens(HIDDEN, BF),
        all_tokens(HIDDEN, F32),
        all_tokens(D, BF),
        all_tokens(HIDDEN, BF),
        all_tokens(D, BF),
        all_tokens(WIDTH, BF),
        all_tokens(3 * WIDTH, BF),
        pltpu.VMEM((4,) + tokens, BF),
        pltpu.VMEM((4,) + tokens, BF),
        pltpu.VMEM(tokens, F32),
        pltpu.VMEM(tokens, F32),
        pltpu.SemaphoreType.DMA((80,)),
        pltpu.SemaphoreType.DMA((80,)),
    ]
    outs = pl.pallas_call(
        main_kernel,
        out_shape=out_shape,
        in_specs=[vmem, smem] + [vmem] * 13,
        out_specs=[vmem] * 14,
        scratch_shapes=scratch,
        compiler_params=pltpu.CompilerParams(
            collective_id=0, has_side_effects=True, vmem_limit_bytes=63 * 2**20
        ),
    )(
        layer_input,
        lengths,
        cotangent,
        norm1_gain,
        norm1_shift,
        qkv_weight.reshape(share, 3 * WIDTH),
        qkv_bias,
        dense_weight[0],
        dense_bias,
        norm2_gain,
        norm2_shift,
        up_weight[0],
        up_bias,
        down_weight[0],
        down_bias,
    )
    (y, gx, n1g, n1s, dqkv, qkvb, ddense, denseb, n2g, n2s, dup, upb, ddown, downb) = outs
    return (
        y[None],
        gx[None],
        n1g,
        n1s,
        dqkv.reshape(1, share, 3, WIDTH),
        qkvb,
        ddense[None],
        denseb,
        n2g,
        n2s,
        dup[None],
        upb,
        ddown[None],
        downb,
    )


def solution(mesh):
    in_specs = (
        P("dp", "tensor", None),
        P("dp", None),
        P("dp", "tensor", None),
        P("section", None),
        P("section", None),
        P("section", "dp", None, "tensor"),
        P("section", None, "tensor"),
        P("section", "dp", "tensor"),
        P("section", None),
        P("section", None),
        P("section", None),
        P("section", "dp", "tensor"),
        P("section", "tensor"),
        P("section", "dp", "tensor"),
        P("section", None),
    )
    out_specs = (
        P("section", "dp", "tensor", None),
        P("section", "dp", "tensor", None),
        P("section", None),
        P("section", None),
        P("section", "dp", None, "tensor"),
        P("section", None, "tensor"),
        P("section", "dp", "tensor"),
        P("section", None),
        P("section", None),
        P("section", None),
        P("section", "dp", "tensor"),
        P("section", "tensor"),
        P("section", "dp", "tensor"),
        P("section", None),
    )
    return jax.shard_map(local, mesh=mesh, in_specs=in_specs, out_specs=out_specs, check_vma=False)
```

```python
import jax
import jax.numpy as jnp
from jax import lax
from jax.experimental import pallas as pl
from jax.experimental.pallas import tpu as pltpu
from jax.sharding import PartitionSpec as P

D = 1024
HEADS = 16
HEAD_DIM = 64
FF = 4096
ROWS = 128
EPSILON = 1e-05
GELU_A = 0.79788456
GELU_B = 0.044715

SEQS = 2
HALF = 64
HEADS_HERE = HEADS // 2
WIDTH = HEADS_HERE * HEAD_DIM
HIDDEN = FF // 2
QKV_AT = 0
DENSE_AT = 3 * WIDTH
UP_AT = DENSE_AT + WIDTH
DOWN_AT = UP_AT + HIDDEN
COLUMNS = DOWN_AT + HIDDEN
TILE = 512
GROUP = 2048
GROUP_QD, GROUP_UP, GROUP_DOWN = 0, 1, 2

BF = jnp.bfloat16
F32 = jnp.float32
MESH = pl.DeviceIdType.MESH

NN = (((1,), (0,)), ((), ()))
NT = (((1,), (1,)), ((), ()))
TN = (((0,), (0,)), ((), ()))


def mm(left, right, dims=NN):
    return lax.dot_general(left, right, dims, preferred_element_type=F32)


class Links:
    def __init__(self, send_sems, recv_sems):
        self.send_sems = send_sems
        self.recv_sems = recv_sems
        self.names = {}
        self.sources = {}

    def index(self, name):
        return self.names.setdefault(name, len(self.names))

    def copy(self, name, src, dst, device):
        i = self.index(name)
        return pltpu.make_async_remote_copy(
            src_ref=src,
            dst_ref=dst,
            send_sem=self.send_sems.at[i],
            recv_sem=self.recv_sems.at[i],
            device_id=device,
            device_id_type=MESH,
        )

    def send(self, name, source, dst, device):
        self.copy(name, source(), dst, device).start()
        self.sources.setdefault(name, source)

    def arrived(self, name, landing, device):
        self.copy(name, landing, landing, device).wait_recv()

    def drain(self, device):
        for name, source in self.sources.items():
            ref = source()
            self.copy(name, ref, ref, device).wait_send()
        self.sources = {}


def four(value):
    return lax.rem(value + 8, 4)


class Place:
    def __init__(self):
        self.section = lax.axis_index("section")
        self.tensor = lax.axis_index("tensor")
        dp = lax.axis_index("dp")
        self.core = lax.rem(dp, 2)
        self.y = lax.rem(lax.div(dp, 2), 4)
        self.z = lax.div(dp, 8)
        self.d = 1 - 2 * self.core
        self.back = -self.d

    def dp(self, z, y, core):
        return {"dp": (z * 4 + y) * 2 + core}

    def along(self, axis, offset):
        if axis == "y":
            return self.dp(self.z, four(self.y + offset), self.core)
        return self.dp(four(self.z + offset), self.y, self.core)

    def sibling(self):
        return self.dp(self.z, self.y, 1 - self.core)

    def peer(self):
        return {"tensor": 1 - self.tensor}

    def other_section(self):
        return {"section": 1 - self.section}


FIRST = ("y", "z")
SECOND = ("z", "y")


def gather_steps(place, links, w, number):
    z, y, core, d, back = place.z, place.y, place.core, place.d, place.back
    cols = pl.ds(number * GROUP, GROUP)
    firsts = (0, back, d, 2)
    halves = range(2)

    def piece(half, first, second):
        if half == 0:
            return w.at[four(z + second), four(y + first), core, 0, :, cols]
        return w.at[four(z + first), four(y + second), core, 1, :, cols]

    def name_of(name, half):
        return ("gather", number, name, half)

    def send(name, half, spot, axis, offset):
        links.send(
            name_of(name, half),
            lambda: piece(half, *spot),
            piece(half, *spot),
            place.along(axis, offset),
        )

    def arrived(name, half, spot):
        links.arrived(name_of(name, half), piece(half, *spot), place.sibling())

    def second_sends(half, k):
        send(("s+", k), half, (firsts[k], 0), SECOND[half], d)
        send(("s-", k), half, (firsts[k], 0), SECOND[half], back)

    def relay(half, k):
        arrived(("s+", k), half, (firsts[k], back))
        send(("sr", k), half, (firsts[k], back), SECOND[half], d)

    def group(half, second, of_core):
        if half == 0:
            return w.at[four(z + second), :, of_core, 0, :, cols]
        return w.at[:, four(y + second), of_core, 1, :, cols]

    def to_sibling(j, second):
        for half in halves:
            links.send(
                name_of(("swap", j), half),
                lambda half=half: group(half, second, core),
                group(half, second, core),
                place.sibling(),
            )

    def step0():
        for half in halves:
            send("f+", half, (0, 0), FIRST[half], d)
            send("f-", half, (0, 0), FIRST[half], back)
        for half in halves:
            second_sends(half, 0)

    def step1():
        for half in halves:
            arrived("f+", half, (back, 0))
            send("fr", half, (back, 0), FIRST[half], d)
            second_sends(half, 1)

    def step2():
        for half in halves:
            arrived("f-", half, (d, 0))
            second_sends(half, 2)
        for half in halves:
            relay(half, 0)

    def step3():
        for half in halves:
            arrived("fr", half, (2, 0))
            second_sends(half, 3)
        to_sibling(0, 0)

    def step4():
        for k in (1, 2):
            for half in halves:
                relay(half, k)

    def step5():
        for half in halves:
            relay(half, 3)
        to_sibling(1, back)

    def step6():
        for k in range(4):
            for half in halves:
                arrived(("s-", k), half, (firsts[k], d))
        to_sibling(2, d)

    def step7():
        for k in range(4):
            for half in halves:
                arrived(("sr", k), half, (firsts[k], 2))
        to_sibling(3, 2)

    def step8():
        for j, second in enumerate((0, d, back, 2)):
            for half in halves:
                links.arrived(
                    name_of(("swap", j), half), group(half, second, 1 - core), place.sibling()
                )

    return (step0, step1, step2, step3, step4, step5, step6, step7, step8)


def scatter_steps(place, links, g, number, sb, r1, r2, r3, q, finish):
    z, y, core, d, back = place.z, place.y, place.core, place.d, place.back
    start = number * GROUP
    all_cols = pl.ds(start, GROUP)
    axes, other_axes = ("z", "y"), ("y", "z")
    spots = (y, z)
    mine, theirs = (0, d, back, 2), (0, back, d, 2)
    halves = range(2)

    def name_of(name, half):
        return ("scatter", number, name, half)

    def group(half, offset, of_core):
        if half == 0:
            return g.at[four(z + offset), :, of_core, 0, :, all_cols]
        return g.at[:, four(y + offset), of_core, 1, :, all_cols]

    def own(half, offset, j):
        if half == 0:
            return g[four(z + offset), j, core, 0, :, all_cols].astype(F32)
        return g[j, four(y + offset), core, 1, :, all_cols].astype(F32)

    def add(half, slot, with_own, *others):
        def one(j, carry):
            total = sb[number, half, slot, j].astype(F32)
            if with_own:
                total = total + own(half, mine[slot], j)
            for other in others:
                total = total + other[number, half, j].astype(F32)
            sb[number, half, slot, j] = total.astype(BF)
            return carry

        lax.fori_loop(0, 4, one, 0)

    def swapped(half, slot):
        links.arrived(name_of(("swap", slot), half), sb.at[number, half, slot], place.sibling())

    def landed(name, half, ref):
        links.arrived(name_of(name, half), ref, place.sibling())

    def step0():
        for slot in (3, 2, 1, 0):
            for half in halves:
                links.send(
                    name_of(("swap", slot), half),
                    lambda slot=slot, half=half: group(half, theirs[slot], 1 - core),
                    sb.at[number, half, slot],
                    place.sibling(),
                )

    def first_send(name, half, slot, to, offset):
        links.send(
            name_of(name, half),
            lambda: sb.at[number, half, slot],
            to.at[number, half],
            place.along(axes[half], offset),
        )

    def step1():
        for half in halves:
            swapped(half, 3)
            add(half, 3, True)
            first_send("r1", half, 3, r1, d)

    def step2():
        for half in halves:
            swapped(half, 2)
            add(half, 2, True)
            first_send("r3", half, 2, r3, back)

    def step3():
        for half in halves:
            swapped(half, 1)
            landed("r1", half, r1.at[number, half])
            add(half, 1, True, r1)
            first_send("r2", half, 1, r2, d)

    def step4():
        for half in halves:
            swapped(half, 0)
            landed("r3", half, r3.at[number, half])
            add(half, 0, True, r3)

    def second_send(name, half, src, to, offset):
        links.send(name_of(name, half), src, to, place.along(other_axes[half], offset))

    def step5():
        for half in halves:
            landed("r2", half, r2.at[number, half])
            add(half, 0, False, r2)
            for name, way, slot, offset in (("q0", 2, 0, d), ("q2", back, 2, back)):
                second_send(
                    name,
                    half,
                    lambda half=half, way=way: sb.at[number, half, 0, four(spots[half] + way)],
                    q.at[number, half, slot],
                    offset,
                )

    def step6():
        for half in halves:
            landed("q0", half, q.at[number, half, 0])
            total = q[number, half, 0].astype(F32)
            total = total + sb[number, half, 0, four(spots[half] + d)].astype(F32)
            q[number, half, 0] = total.astype(BF)
            second_send(
                "q1", half, lambda half=half: q.at[number, half, 0], q.at[number, half, 1], d
            )

    def step7():
        for half in halves:
            landed("q2", half, q.at[number, half, 2])
            landed("q1", half, q.at[number, half, 1])

            def value(at):
                cols = pl.ds(at, TILE)
                return (
                    sb[number, half, 0, spots[half], :, cols].astype(F32)
                    + q[number, half, 1, :, cols].astype(F32)
                    + q[number, half, 2, :, cols].astype(F32)
                )

            finish(slice(half * 16, half * 16 + 16), value)

    return (step0, step1, step2, step3, step4, step5, step6, step7)


def small_steps(place, links, small, small_in):
    z, y, core = place.z, place.y, place.core
    partners = (
        place.peer(),
        place.sibling(),
        place.dp(z, y + 1 - 2 * lax.rem(y, 2), core),
        place.dp(z, 3 - y, core),
        place.dp(z + 1 - 2 * lax.rem(z, 2), y, core),
        place.dp(3 - z, y, core),
    )

    def rows_of(step):
        return pl.ds(0, 8 if step == 0 else 16)

    def begin(step):
        rows = rows_of(step)
        links.send(
            ("small", step),
            lambda: small.at[step, rows],
            small_in.at[step, rows],
            partners[step],
        )

    def end(step):
        links.arrived(("small", step), small_in.at[step, rows_of(step)], partners[step])
        if step == 0:
            small[1, 0:8] = small[0, 0:8] + small_in[0, 0:8]
            small[1, 8:16] = small[0, 8:16]
        else:
            small[step + 1] = small[step] + small_in[step]

    def at(step):
        def run():
            if step > 0:
                end(step - 1)
            if step < 6:
                begin(step)

        return run

    return tuple(at(step) for step in range(7))


def normalise(values):
    mean = jnp.mean(values, axis=-1, keepdims=True)
    centred = values - mean
    inverse = lax.rsqrt(jnp.mean(centred * centred, axis=-1, keepdims=True) + EPSILON)
    return centred * inverse, inverse


def normalise_back(grad, normed, inverse, gain):
    scaled = grad * gain
    one = jnp.mean(scaled, axis=-1, keepdims=True)
    two = jnp.mean(scaled * normed, axis=-1, keepdims=True)
    return inverse * (scaled - one - normed * two)


def column_sum(values):
    return jnp.sum(values, axis=0, keepdims=True)


def whole_columns(w, cols):
    return w[:, :, :, :, :, cols].reshape(D, -1)


def weight_grad(g, left, right, start, count):
    def one(i, carry):
        at = pl.multiple_of(i * 256, 256)
        piece = left[:, :, :, pl.ds(at, 256)].reshape(SEQS * ROWS, 256)
        for col in range(0, count, TILE):
            size = min(TILE, count - col)
            part = right[:, :, :, col : col + size].reshape(SEQS * ROWS, size)
            value = mm(piece, part, TN).astype(BF)
            g[i, :, :, :, :, start + col : start + col + size] = value.reshape(4, 2, 2, 16, size)
        return carry

    lax.fori_loop(0, 4, one, 0)


def score_bias(lengths, seq):
    queries = lax.broadcasted_iota(jnp.int32, (ROWS, ROWS), 0)
    keys = lax.broadcasted_iota(jnp.int32, (ROWS, ROWS), 1)
    query_segment = jnp.zeros((ROWS, ROWS), jnp.int32)
    key_segment = jnp.zeros((ROWS, ROWS), jnp.int32)
    end = 0
    for doc in range(4):
        end = end + lengths[seq, doc]
        query_segment = query_segment + (queries >= end).astype(jnp.int32)
        key_segment = key_segment + (keys >= end).astype(jnp.int32)
    allowed = (query_segment == key_segment) & (keys <= queries)
    return jnp.where(allowed, 0.0, -1e30), (queries - keys).astype(F32)


def halves_of_pair():
    lanes = lax.broadcasted_iota(jnp.int32, (1, 128), 1).astype(F32)
    low = jnp.where(lanes < HEAD_DIM, 1.0, 0.0).astype(BF)
    high = jnp.where(lanes < HEAD_DIM, 0.0, 1.0).astype(BF)
    return low, high


def main_kernel(
    x_ref, lengths, cot_ref, n1g, n1s, wqkv, qkvb, wdense, denseb, n2g, n2s, wup, upb, wdown, downb,
    y_out, gx_out, dn1g, dn1s, dqkv, dqkvb, ddense, ddenseb, dn2g, dn2s, dup, dupb, ddown, ddownb,
    w, g, sb, r1, r2, r3, q, small, small_in,
    xs, inbox, outbox, a_all, qkv, o_all, p_all, hidden, xh1, xh2, inv1, inv2, c_all, act, slope_u,
    gz_all, gu, gat_all, go, gqkv, part_out, part_in, wide, ghid, send_sems, recv_sems,
):
    place = Place()
    links = Links(send_sems, recv_sems)
    t, other = place.tensor, 1 - place.tensor
    streams = range(SEQS)

    def at_section(number, *steps):
        @pl.when(place.section == number)
        def _():
            for step in steps:
                step()

    barrier = pltpu.get_barrier_semaphore()
    neighbours = [
        place.along("y", 1),
        place.along("y", -1),
        place.along("z", 1),
        place.along("z", -1),
        place.sibling(),
        place.peer(),
        place.other_section(),
    ]
    for neighbour in neighbours:
        pl.semaphore_signal(barrier, inc=1, device_id=neighbour, device_id_type=MESH)
    for half in range(2):
        rows = slice(half * 16, half * 16 + 16)
        here = w.at[place.z, place.y, place.core, half]
        for kind in range(3):
            here[:, kind * WIDTH : (kind + 1) * WIDTH] = wqkv[0, kind, rows, :]
        for ref, start in ((wdense, DENSE_AT), (wup, UP_AT), (wdown, DOWN_AT)):
            here[:, start : start + ref.shape[2]] = ref[0, rows, :]
    pl.semaphore_wait(barrier, len(neighbours))

    def share(name, ref, s):
        links.send((name, s), lambda: ref.at[s, t], ref.at[s, t], place.peer())

    def shared(name, ref, s):
        links.arrived((name, s), ref.at[s, other], place.peer())

    def partial(name, k, s, start, count, source):
        rows = jnp.concatenate([source[s, other], source[s, t]], axis=0)

        def one(i, carry):
            cols = pl.ds(pl.multiple_of(i * 256, 256), 256)
            value = mm(rows, w[i, :, :, :, :, start : start + count].reshape(256, count), NT)
            part_out[k, s, :, cols] = value[:HALF].astype(BF)
            wide[k % 2, s, :, cols] = value[HALF:]
            return carry

        lax.fori_loop(0, 4, one, 0)
        links.send((name, s), lambda: part_out.at[k, s], part_in.at[k, s], place.peer())

    def summed(name, k, s):
        links.arrived((name, s), part_in.at[k, s], place.peer())
        return wide[k % 2, s] + part_in[k, s].astype(F32)

    gather = [gather_steps(place, links, w, number) for number in range(3)]

    def all_gathers():
        for step in range(9):
            for number in range(3):
                gather[number][step]()

    def cotangent_shared():
        for s in streams:
            gz_all[s, t] = cot_ref[s]
            share("gz", gz_all, s)

    qd, up, down = gather
    at_section(1, all_gathers, cotangent_shared)
    at_section(0, *qd[0:5], up[0], *qd[5:8], up[1], qd[8])

    gain1, shift1 = n1g[...].astype(F32), n1s[...].astype(F32)
    gain2, shift2 = n2g[...].astype(F32), n2s[...].astype(F32)
    masks = halves_of_pair()
    tensor_scale = jnp.where(t == 0, 1.0, 2.0 ** (-8.0 * HEADS_HERE / HEADS))

    def enter(s):
        @pl.when(place.section == 0)
        def _():
            xs[s] = x_ref[s]

        @pl.when(place.section == 1)
        def _():
            links.arrived(("forward", s), inbox.at[s], place.other_section())
            xs[s] = inbox[s]

        normed, inverse = normalise(xs[s].astype(F32))
        xh1[s] = normed
        inv1[s] = jnp.broadcast_to(inverse, (HALF, 128))
        a_all[s, t] = (normed * gain1 + shift1).astype(BF)
        share("a", a_all, s)

    def project(s):
        shared("a", a_all, s)
        rows = a_all[s].reshape(ROWS, D)
        for kind in range(3):
            cols = slice(kind * WIDTH, (kind + 1) * WIDTH)
            value = mm(rows, whole_columns(w, cols)) + qkvb[0, kind : kind + 1].astype(F32)
            qkv[s, :, :, cols] = value.astype(BF).reshape(2, HALF, WIDTH)

    def heads_of(ref, s, kind, pair):
        at = kind * WIDTH + pair * 128
        return ref[s, :, :, at : at + 128].reshape(ROWS, 128)

    def attend(s):
        bias, distance = score_bias(lengths, s)
        distance = distance * tensor_scale
        for pair in range(HEADS_HERE // 2):
            queries, keys, values = (heads_of(qkv, s, kind, pair) for kind in range(3))
            mixed = None
            for side in range(2):
                head = pair * 2 + side
                slope = 2.0 ** (-8.0 * (head + 1) / HEADS)
                scores = mm(queries * masks[side], keys, NT) * HEAD_DIM ** (-0.5)
                scores = scores + (bias - slope * distance)
                exponent = jnp.exp(scores - jnp.max(scores, axis=-1, keepdims=True))
                chances = exponent / jnp.sum(exponent, axis=-1, keepdims=True)
                p_all[s, head] = chances
                term = mm(chances.astype(BF), values * masks[side])
                mixed = term if mixed is None else mixed + term
            cols = slice(pair * 128, pair * 128 + 128)
            o_all[s, :, :, cols] = mixed.astype(BF).reshape(2, HALF, 128)
        partial("attended", 0, s, DENSE_AT, WIDTH, o_all)

    def middle(s):
        value = xs[s].astype(F32) + denseb[...].astype(F32)
        value = value + summed("attended", 0, s)
        hidden[s] = value
        normed, inverse = normalise(value)
        xh2[s] = normed
        inv2[s] = jnp.broadcast_to(inverse, (HALF, 128))
        c_all[s, t] = (normed * gain2 + shift2).astype(BF)
        share("c", c_all, s)

    def expand(s):
        shared("c", c_all, s)
        rows = c_all[s].reshape(ROWS, D)

        def one(i, carry):
            at = pl.multiple_of(i * TILE, TILE)
            u = mm(rows, whole_columns(w, pl.ds(UP_AT + at, TILE)))
            u = u + upb[:, pl.ds(at, TILE)].astype(F32)
            square = u * u
            tanh = jnp.tanh(GELU_A * u * (1.0 + GELU_B * square))
            inner = GELU_A * (1.0 + (3.0 * GELU_B) * square)
            value = (0.5 * u * (1.0 + tanh)).astype(BF)
            act[s, :, :, pl.ds(at, TILE)] = value.reshape(2, HALF, TILE)
            slope = 0.5 * (1.0 + tanh) + 0.5 * u * (1.0 - tanh * tanh) * inner
            slope_u[s, :, :, pl.ds(at, TILE)] = slope.reshape(2, HALF, TILE)
            return carry

        lax.fori_loop(0, HIDDEN // TILE, one, 0)

    def contract(s):
        partial("lowered", 1, s, DOWN_AT, HIDDEN, act)

    def leave(s):
        value = hidden[s] + downb[...].astype(F32) + summed("lowered", 1, s)
        outbox[0, s] = value.astype(BF)
        y_out[0, s] = value.astype(BF)

    def forward_copy(s):
        return links.copy(("forward", s), outbox.at[0, s], inbox.at[s], place.other_section())

    def backward_copy(s):
        return links.copy(("backward", s), outbox.at[1, s], inbox.at[s], place.other_section())

    enter(0)
    enter(1)
    at_section(0, up[2], up[3])
    project(0)
    at_section(0, up[4], up[5], down[0])
    attend(0)
    at_section(0, up[6], up[7], down[1])
    project(1)
    at_section(0, up[8], down[2], down[3])
    attend(1)
    at_section(0, down[4], down[5])
    middle(0)
    middle(1)
    at_section(0, down[6], down[7])
    expand(0)
    at_section(0, down[8])
    contract(0)
    expand(1)
    contract(1)

    @pl.when(place.section == 0)
    def _():
        for s in streams:
            leave(s)
            forward_copy(s).start()

    @pl.when(place.section == 0)
    def _():
        for s in streams:
            links.arrived(("backward", s), inbox.at[s], place.other_section())
            gz_all[s, t] = inbox[s]
            share("gz", gz_all, s)

    sums = [0.0] * 6

    def contract_back(s):
        shared("gz", gz_all, s)
        rows = gz_all[s].reshape(ROWS, D)

        def one(i, carry):
            at = pl.multiple_of(i * TILE, TILE)
            value = mm(rows, whole_columns(w, pl.ds(DOWN_AT + at, TILE)))
            value = value * slope_u[s, :, :, pl.ds(at, TILE)].reshape(ROWS, TILE)
            gu[s, :, :, pl.ds(at, TILE)] = value.astype(BF).reshape(2, HALF, TILE)
            return carry

        lax.fori_loop(0, HIDDEN // TILE, one, 0)
        partial("gc", 2, s, UP_AT, HIDDEN, gu)

    def middle_back(s):
        grad = summed("gc", 2, s)
        normed = xh2[s]
        gy = gz_all[s, t].astype(F32)
        sums[3] = sums[3] + column_sum(grad * normed)
        sums[4] = sums[4] + column_sum(grad)
        sums[5] = sums[5] + column_sum(gy)
        value = gy + normalise_back(grad, normed, inv2[s][:, 0:1], gain2)
        ghid[s] = value
        sums[2] = sums[2] + column_sum(value)
        gat_all[s, t] = value.astype(BF)
        share("gat", gat_all, s)

    def attend_back(s):
        shared("gat", gat_all, s)
        rows = gat_all[s].reshape(ROWS, D)
        value = mm(rows, whole_columns(w, slice(DENSE_AT, DENSE_AT + WIDTH)))
        go[s] = value.astype(BF).reshape(2, HALF, WIDTH)
        for pair in range(HEADS_HERE // 2):
            queries, keys, values = (heads_of(qkv, s, kind, pair) for kind in range(3))
            grads = heads_of(go, s, 0, pair)
            totals = [None, None, None]
            for side in range(2):
                chances = p_all[s, pair * 2 + side]
                out_grad = grads * masks[side]
                chance_grad = mm(out_grad, values, NT)
                inner = jnp.sum(chances * chance_grad, axis=-1, keepdims=True)
                score_grad = (chances * (chance_grad - inner)).astype(BF)
                terms = (
                    mm(score_grad, keys * masks[side]),
                    mm(score_grad, queries * masks[side], TN),
                    mm(chances.astype(BF), out_grad, TN),
                )
                totals = [b if a is None else a + b for a, b in zip(totals, terms)]
            scale = HEAD_DIM ** (-0.5)
            for kind, value in enumerate((totals[0] * scale, totals[1] * scale, totals[2])):
                at = kind * WIDTH + pair * 128
                gqkv[s, :, :, at : at + 128] = value.astype(BF).reshape(2, HALF, 128)
        partial("ga", 4, s, QKV_AT, 3 * WIDTH, gqkv)

    def leave_back(s):
        grad = summed("ga", 4, s)
        normed = xh1[s]
        sums[0] = sums[0] + column_sum(grad * normed)
        sums[1] = sums[1] + column_sum(grad)
        value = ghid[s] + normalise_back(grad, normed, inv1[s][:, 0:1], gain1)
        outbox[1, s] = value.astype(BF)
        gx_out[0, s] = value.astype(BF)

        @pl.when(place.section == 1)
        def _():
            backward_copy(s).start()

    def finish_qd(rows, value):
        for kind in range(3):
            dqkv[0, kind, rows, :] = value(kind * WIDTH)
        ddense[0, rows, :] = value(DENSE_AT)

    def finish_into(out):
        def finish(rows, value):
            for at in range(0, GROUP, TILE):
                out[0, rows, at : at + TILE] = value(at)

        return finish

    finishes = (finish_qd, finish_into(dup), finish_into(ddown))
    sc_qd, sc_up, sc_down = (
        scatter_steps(place, links, g, number, sb, r1, r2, r3, q, finishes[number])
        for number in range(3)
    )

    def grad_down():
        weight_grad(g, gz_all, act, DOWN_AT, HIDDEN)

    def grad_up():
        weight_grad(g, c_all, gu, UP_AT, HIDDEN)

    contract_back(0)
    contract_back(1)
    at_section(1, lambda: leave(0), lambda: leave(1))
    middle_back(0)
    grad_down()
    at_section(0, sc_down[0])
    middle_back(1)
    at_section(0, grad_up, sc_up[0], sc_down[1])
    attend_back(0)
    at_section(0, sc_down[2], sc_up[1], sc_down[3])
    attend_back(1)
    at_section(0, sc_up[2], sc_down[4], sc_up[3], sc_down[5])
    leave_back(0)
    at_section(0, sc_up[4], sc_down[6])
    leave_back(1)
    at_section(0, sc_up[5], sc_down[7])
    at_section(1, grad_up)
    weight_grad(g, a_all, gqkv, QKV_AT, 3 * WIDTH)
    weight_grad(g, gat_all, o_all, DENSE_AT, WIDTH)
    at_section(0, sc_qd[0], sc_up[6], sc_up[7])

    small[0, 6:8] = jnp.zeros((2, D), F32)
    small[0, 12:16] = jnp.zeros((4, D), F32)
    for row in range(6):
        small[0, row : row + 1] = sums[row]
    for i in range(2):
        piece = gu[:, :, :, i * D : (i + 1) * D].reshape(SEQS * ROWS, D).astype(F32)
        small[0, 8 + i : 9 + i] = column_sum(piece)
    piece = gqkv[:, :, :, 0:D].reshape(SEQS * ROWS, D).astype(F32)
    small[0, 10:11] = column_sum(piece)
    piece = gqkv[:, :, :, D : 3 * WIDTH].reshape(SEQS * ROWS, WIDTH).astype(F32)
    small[0, 11:12, 0:WIDTH] = column_sum(piece)
    small[0, 11:12, WIDTH:D] = jnp.zeros((1, D - WIDTH), F32)

    tiny = small_steps(place, links, small, small_in)
    last = []
    for step in range(1, 8):
        last += [tiny[step - 1], sc_qd[step]]
    at_section(0, *last)
    last = [sc_down[0], sc_up[0], sc_qd[0]]
    for step in range(1, 8):
        last += [tiny[step - 1], sc_down[step], sc_up[step], sc_qd[step]]
    at_section(1, *last)

    for row, out in enumerate((dn1g, dn1s, ddenseb, dn2g, dn2s, ddownb)):
        out[...] = small[6, row : row + 1]
    dupb[:, 0:D] = small[6, 8:9]
    dupb[:, D : 2 * D] = small[6, 9:10]
    dqkvb[0] = small[6, 10:11, 0:WIDTH]
    dqkvb[1] = small[6, 10:11, WIDTH : 2 * WIDTH]
    dqkvb[2] = small[6, 11:12, 0:WIDTH]

    links.drain(place.sibling())
    at_section(0, *(forward_copy(s).wait_send for s in streams))
    at_section(1, *(backward_copy(s).wait_send for s in streams))


def publish_kernel(*refs):
    count = len(refs) // 2
    sems = refs[-1]
    copies = [pltpu.make_async_copy(refs[i], refs[count + i], sems.at[i]) for i in range(count)]
    for copy in copies:
        copy.start()
    for copy in copies:
        copy.wait()


def local(
    layer_input,
    lengths,
    cotangent,
    norm1_gain,
    norm1_shift,
    qkv_weight,
    qkv_bias,
    dense_weight,
    dense_bias,
    norm2_gain,
    norm2_shift,
    up_weight,
    up_bias,
    down_weight,
    down_bias,
):
    share = qkv_weight.shape[1]
    vmem = pl.BlockSpec(memory_space=pltpu.VMEM)
    smem = pl.BlockSpec(memory_space=pltpu.SMEM)
    shape = jax.ShapeDtypeStruct
    tokens = (SEQS, HALF, D)
    tokens_out = shape((1,) + tokens, BF)
    row = shape((1, D), F32)
    out_shape = (
        tokens_out,
        tokens_out,
        row,
        row,
        shape((1, 3, share, WIDTH), F32),
        shape((3, 1, WIDTH), F32),
        shape((1, share, WIDTH), F32),
        row,
        row,
        row,
        shape((1, share, HIDDEN), F32),
        shape((1, HIDDEN), F32),
        shape((1, share, HIDDEN), F32),
        row,
    )
    block = (4, 4, 2, 2, 16, COLUMNS)

    def all_tokens(width, dtype):
        return pltpu.VMEM((SEQS, 2, HALF, width), dtype)

    scratch = [
        pltpu.VMEM(block, BF),
        pltpu.VMEM(block, BF),
        pltpu.VMEM((3, 2, 4, 4, 16, GROUP), BF),
        pltpu.VMEM((3, 2, 4, 16, GROUP), BF),
        pltpu.VMEM((3, 2, 4, 16, GROUP), BF),
        pltpu.VMEM((3, 2, 4, 16, GROUP), BF),
        pltpu.VMEM((3, 2, 3, 16, GROUP), BF),
        pltpu.VMEM((7, 16, D), F32),
        pltpu.VMEM((6, 16, D), F32),
        pltpu.VMEM(tokens, BF),
        pltpu.VMEM(tokens, BF),
        pltpu.VMEM((2,) + tokens, BF),
        all_tokens(D, BF),
        all_tokens(3 * WIDTH, BF),
        all_tokens(WIDTH, BF),
        pltpu.VMEM((SEQS, HEADS_HERE, ROWS, ROWS), F32),
        pltpu.VMEM(tokens, F32),
        pltpu.VMEM(tokens, F32),
        pltpu.VMEM(tokens, F32),
        pltpu.VMEM((SEQS, HALF, 128), F32),
        pltpu.VMEM((SEQS, HALF, 128), F32),
        all_tokens(D, BF),
        all_tokens(HIDDEN, BF),
        all_tokens(HIDDEN, F32),
        all_tokens(D, BF),
        all_tokens(HIDDEN, BF),
        all_tokens(D, BF),
        all_tokens(WIDTH, BF),
        all_tokens(3 * WIDTH, BF),
        pltpu.VMEM((5,) + tokens, BF),
        pltpu.VMEM((5,) + tokens, BF),
        pltpu.VMEM((2,) + tokens, F32),
        pltpu.VMEM(tokens, F32),
        pltpu.SemaphoreType.DMA((208,)),
        pltpu.SemaphoreType.DMA((208,)),
    ]
    outs = pl.pallas_call(
        main_kernel,
        out_shape=out_shape,
        in_specs=[vmem, smem] + [vmem] * 13,
        out_specs=[vmem] * 14,
        scratch_shapes=scratch,
        compiler_params=pltpu.CompilerParams(
            collective_id=0, has_side_effects=True, vmem_limit_bytes=63 * 2**20
        ),
    )(
        layer_input,
        lengths,
        cotangent,
        norm1_gain,
        norm1_shift,
        jnp.transpose(qkv_weight, (0, 2, 1, 3)),
        qkv_bias,
        dense_weight,
        dense_bias,
        norm2_gain,
        norm2_shift,
        up_weight,
        up_bias,
        down_weight,
        down_bias,
    )
    outs = pl.pallas_call(
        publish_kernel,
        out_shape=out_shape,
        in_specs=[pl.BlockSpec(memory_space=pl.ANY)] * 14,
        out_specs=[vmem] * 14,
        scratch_shapes=[pltpu.SemaphoreType.DMA((14,))],
        compiler_params=pltpu.CompilerParams(vmem_limit_bytes=62 * 2**20),
    )(*outs)
    outs = list(outs)
    outs[4] = jnp.transpose(outs[4], (0, 2, 1, 3))
    outs[5] = jnp.transpose(outs[5], (1, 0, 2))
    return tuple(outs)


def solution(mesh):
    in_specs = (
        P("dp", "tensor", None),
        P("dp", None),
        P("dp", "tensor", None),
        P("section", None),
        P("section", None),
        P("section", "dp", None, "tensor"),
        P("section", None, "tensor"),
        P("section", "dp", "tensor"),
        P("section", None),
        P("section", None),
        P("section", None),
        P("section", "dp", "tensor"),
        P("section", "tensor"),
        P("section", "dp", "tensor"),
        P("section", None),
    )
    out_specs = (
        P("section", "dp", "tensor", None),
        P("section", "dp", "tensor", None),
        P("section", None),
        P("section", None),
        P("section", "dp", None, "tensor"),
        P("section", None, "tensor"),
        P("section", "dp", "tensor"),
        P("section", None),
        P("section", None),
        P("section", None),
        P("section", "dp", "tensor"),
        P("section", "tensor"),
        P("section", "dp", "tensor"),
        P("section", None),
    )
    return jax.shard_map(local, mesh=mesh, in_specs=in_specs, out_specs=out_specs, check_vma=False)
```

```python
import jax
import jax.numpy as jnp
from jax import lax
from jax.experimental import pallas as pl
from jax.experimental.pallas import tpu as pltpu
from jax.sharding import PartitionSpec as P

D = 1024
HEADS = 16
HEAD_DIM = 64
FF = 4096
ROWS = 128
EPSILON = 1e-05
GELU_A = 0.79788456
GELU_B = 0.044715

SEQS = 2
HALF = 64
HEADS_HERE = HEADS // 2
WIDTH = HEADS_HERE * HEAD_DIM
HIDDEN = FF // 2
QKV_AT = 0
DENSE_AT = 3 * WIDTH
UP_AT = DENSE_AT + WIDTH
DOWN_AT = UP_AT + HIDDEN
COLUMNS = DOWN_AT + HIDDEN
TILE = 512
GROUP = 2048
GROUP_QD, GROUP_UP, GROUP_DOWN = 0, 1, 2

BF = jnp.bfloat16
F32 = jnp.float32
MESH = pl.DeviceIdType.MESH

NN = (((1,), (0,)), ((), ()))
NT = (((1,), (1,)), ((), ()))
TN = (((0,), (0,)), ((), ()))


def mm(left, right, dims=NN):
    return lax.dot_general(left, right, dims, preferred_element_type=F32)


class Links:
    def __init__(self, send_sems, recv_sems):
        self.send_sems = send_sems
        self.recv_sems = recv_sems
        self.names = {}
        self.sources = {}

    def index(self, name):
        return self.names.setdefault(name, len(self.names))

    def copy(self, name, src, dst, device):
        i = self.index(name)
        return pltpu.make_async_remote_copy(
            src_ref=src,
            dst_ref=dst,
            send_sem=self.send_sems.at[i],
            recv_sem=self.recv_sems.at[i],
            device_id=device,
            device_id_type=MESH,
        )

    def send(self, name, source, dst, device):
        self.copy(name, source(), dst, device).start()
        self.sources.setdefault(name, source)

    def arrived(self, name, landing, device):
        self.copy(name, landing, landing, device).wait_recv()

    def drain(self, device):
        for name, source in self.sources.items():
            ref = source()
            self.copy(name, ref, ref, device).wait_send()
        self.sources = {}


def four(value):
    return lax.rem(value + 8, 4)


class Place:
    def __init__(self):
        self.section = lax.axis_index("section")
        self.tensor = lax.axis_index("tensor")
        dp = lax.axis_index("dp")
        self.core = lax.rem(dp, 2)
        self.y = lax.rem(lax.div(dp, 2), 4)
        self.z = lax.div(dp, 8)
        self.d = 1 - 2 * self.core
        self.back = -self.d

    def dp(self, z, y, core):
        return {"dp": (z * 4 + y) * 2 + core}

    def along(self, axis, offset):
        if axis == "y":
            return self.dp(self.z, four(self.y + offset), self.core)
        return self.dp(four(self.z + offset), self.y, self.core)

    def sibling(self):
        return self.dp(self.z, self.y, 1 - self.core)

    def peer(self):
        return {"tensor": 1 - self.tensor}

    def other_section(self):
        return {"section": 1 - self.section}


FIRST = ("y", "z")
SECOND = ("z", "y")


def gather_steps(place, links, w, number):
    z, y, core, d, back = place.z, place.y, place.core, place.d, place.back
    cols = pl.ds(number * GROUP, GROUP)
    firsts = (0, back, d, 2)
    halves = range(2)

    def piece(half, first, second):
        if half == 0:
            return w.at[four(z + second), four(y + first), core, 0, :, cols]
        return w.at[four(z + first), four(y + second), core, 1, :, cols]

    def name_of(name, half):
        return ("gather", number, name, half)

    def send(name, half, spot, axis, offset):
        links.send(
            name_of(name, half),
            lambda: piece(half, *spot),
            piece(half, *spot),
            place.along(axis, offset),
        )

    def arrived(name, half, spot):
        links.arrived(name_of(name, half), piece(half, *spot), place.sibling())

    def second_sends(half, k):
        send(("s+", k), half, (firsts[k], 0), SECOND[half], d)
        send(("s-", k), half, (firsts[k], 0), SECOND[half], back)

    def relay(half, k):
        arrived(("s+", k), half, (firsts[k], back))
        send(("sr", k), half, (firsts[k], back), SECOND[half], d)

    def group(half, second, of_core):
        if half == 0:
            return w.at[four(z + second), :, of_core, 0, :, cols]
        return w.at[:, four(y + second), of_core, 1, :, cols]

    def to_sibling(j, second):
        for half in halves:
            links.send(
                name_of(("swap", j), half),
                lambda half=half: group(half, second, core),
                group(half, second, core),
                place.sibling(),
            )

    def step0():
        for half in halves:
            send("f+", half, (0, 0), FIRST[half], d)
            send("f-", half, (0, 0), FIRST[half], back)
        for half in halves:
            second_sends(half, 0)

    def step1():
        for half in halves:
            arrived("f+", half, (back, 0))
            send("fr", half, (back, 0), FIRST[half], d)
            second_sends(half, 1)

    def step2():
        for half in halves:
            arrived("f-", half, (d, 0))
            second_sends(half, 2)
        for half in halves:
            relay(half, 0)

    def step3():
        for half in halves:
            arrived("fr", half, (2, 0))
            second_sends(half, 3)
        to_sibling(0, 0)

    def step4():
        for k in (1, 2):
            for half in halves:
                relay(half, k)

    def step5():
        for half in halves:
            relay(half, 3)
        to_sibling(1, back)

    def step6():
        for k in range(4):
            for half in halves:
                arrived(("s-", k), half, (firsts[k], d))
        to_sibling(2, d)

    def step7():
        for k in range(4):
            for half in halves:
                arrived(("sr", k), half, (firsts[k], 2))
        to_sibling(3, 2)

    def step8():
        for j, second in enumerate((0, d, back, 2)):
            for half in halves:
                links.arrived(
                    name_of(("swap", j), half), group(half, second, 1 - core), place.sibling()
                )

    return (step0, step1, step2, step3, step4, step5, step6, step7, step8)


def scatter_steps(place, links, g, start, count, sb, r1, r2, r3, q, finish):
    z, y, core, d, back = place.z, place.y, place.core, place.d, place.back
    all_cols = pl.ds(start, count)
    axes, other_axes = ("z", "y"), ("y", "z")
    spots = (y, z)
    mine, theirs = (0, d, back, 2), (0, back, d, 2)
    halves = range(2)

    def name_of(name, half):
        return ("scatter", start, name, half)

    def group(half, offset, of_core):
        if half == 0:
            return g.at[four(z + offset), :, of_core, 0, :, all_cols]
        return g.at[:, four(y + offset), of_core, 1, :, all_cols]

    def own(half, offset, j):
        if half == 0:
            return g[four(z + offset), j, core, 0, :, all_cols].astype(F32)
        return g[j, four(y + offset), core, 1, :, all_cols].astype(F32)

    def add(half, slot, with_own, *others):
        for j in range(4):
            total = sb[half, slot, j, :, all_cols].astype(F32)
            if with_own:
                total = total + own(half, mine[slot], j)
            for other in others:
                total = total + other[half, j, :, all_cols].astype(F32)
            sb[half, slot, j, :, all_cols] = total.astype(BF)

    def swapped(half, slot):
        links.arrived(name_of(("swap", slot), half), sb.at[half, slot, :, :, all_cols], place.sibling())

    def landed(name, half, ref):
        links.arrived(name_of(name, half), ref, place.sibling())

    def step0():
        for slot in (3, 2, 1, 0):
            for half in halves:
                links.send(
                    name_of(("swap", slot), half),
                    lambda slot=slot, half=half: group(half, theirs[slot], 1 - core),
                    sb.at[half, slot, :, :, all_cols],
                    place.sibling(),
                )

    def first_send(name, half, slot, to, offset):
        links.send(
            name_of(name, half),
            lambda: sb.at[half, slot, :, :, all_cols],
            to.at[half, :, :, all_cols],
            place.along(axes[half], offset),
        )

    def step1():
        for half in halves:
            swapped(half, 3)
            add(half, 3, True)
            first_send("r1", half, 3, r1, d)

    def step2():
        for half in halves:
            swapped(half, 2)
            add(half, 2, True)
            first_send("r3", half, 2, r3, back)

    def step3():
        for half in halves:
            swapped(half, 1)
            landed("r1", half, r1.at[half, :, :, all_cols])
            add(half, 1, True, r1)
            first_send("r2", half, 1, r2, d)

    def step4():
        for half in halves:
            swapped(half, 0)
            landed("r3", half, r3.at[half, :, :, all_cols])
            add(half, 0, True, r3)

    def second_send(name, half, src, to, offset):
        links.send(name_of(name, half), src, to, place.along(other_axes[half], offset))

    def step5():
        for half in halves:
            landed("r2", half, r2.at[half, :, :, all_cols])
            add(half, 0, False, r2)
            for name, way, slot, offset in (("q0", 2, 0, d), ("q2", back, 2, back)):
                second_send(
                    name,
                    half,
                    lambda half=half, way=way: sb.at[half, 0, four(spots[half] + way), :, all_cols],
                    q.at[half, slot, :, all_cols],
                    offset,
                )

    def step6():
        for half in halves:
            landed("q0", half, q.at[half, 0, :, all_cols])
            total = q[half, 0, :, all_cols].astype(F32)
            total = total + sb[half, 0, four(spots[half] + d), :, all_cols].astype(F32)
            q[half, 0, :, all_cols] = total.astype(BF)
            second_send(
                "q1", half, lambda half=half: q.at[half, 0, :, all_cols], q.at[half, 1, :, all_cols], d
            )

    def step7():
        for half in halves:
            landed("q2", half, q.at[half, 2, :, all_cols])
            landed("q1", half, q.at[half, 1, :, all_cols])

            def value(at):
                cols = pl.ds(start + at, TILE)
                return (
                    sb[half, 0, spots[half], :, cols].astype(F32)
                    + q[half, 1, :, cols].astype(F32)
                    + q[half, 2, :, cols].astype(F32)
                )

            finish(slice(half * 16, half * 16 + 16), value)

    return (step0, step1, step2, step3, step4, step5, step6, step7)


def small_steps(place, links, small, small_in):
    z, y, core = place.z, place.y, place.core
    partners = (
        place.peer(),
        place.sibling(),
        place.dp(z, y + 1 - 2 * lax.rem(y, 2), core),
        place.dp(z, 3 - y, core),
        place.dp(z + 1 - 2 * lax.rem(z, 2), y, core),
        place.dp(3 - z, y, core),
    )

    def rows_of(step):
        return pl.ds(0, 8 if step == 0 else 16)

    def begin(step):
        rows = rows_of(step)
        links.send(
            ("small", step),
            lambda: small.at[step, rows],
            small_in.at[step, rows],
            partners[step],
        )

    def end(step):
        links.arrived(("small", step), small_in.at[step, rows_of(step)], partners[step])
        if step == 0:
            small[1, 0:8] = small[0, 0:8] + small_in[0, 0:8]
            small[1, 8:16] = small[0, 8:16]
        else:
            small[step + 1] = small[step] + small_in[step]

    def at(step):
        def run():
            if step > 0:
                end(step - 1)
            if step < 6:
                begin(step)

        return run

    return tuple(at(step) for step in range(7))


def normalise(values):
    mean = jnp.mean(values, axis=-1, keepdims=True)
    centred = values - mean
    inverse = lax.rsqrt(jnp.mean(centred * centred, axis=-1, keepdims=True) + EPSILON)
    return centred * inverse, inverse


def normalise_back(grad, normed, inverse, gain):
    scaled = grad * gain
    one = jnp.mean(scaled, axis=-1, keepdims=True)
    two = jnp.mean(scaled * normed, axis=-1, keepdims=True)
    return inverse * (scaled - one - normed * two)


def column_sum(values):
    return jnp.sum(values, axis=0, keepdims=True)


def whole_columns(w, cols):
    return w[:, :, :, :, :, cols].reshape(D, -1)


def weight_grad(g, left, right, start, count):
    for i in range(4):
        piece = left[:, :, :, i * 256 : (i + 1) * 256].reshape(SEQS * ROWS, 256)
        for col in range(0, count, TILE):
            part = right[:, :, :, col : col + TILE].reshape(SEQS * ROWS, TILE)
            value = mm(piece, part, TN).astype(BF)
            g[i, :, :, :, :, start + col : start + col + TILE] = value.reshape(4, 2, 2, 16, TILE)


def score_bias(lengths, seq):
    queries = lax.broadcasted_iota(jnp.int32, (ROWS, ROWS), 0)
    keys = lax.broadcasted_iota(jnp.int32, (ROWS, ROWS), 1)
    query_segment = jnp.zeros((ROWS, ROWS), jnp.int32)
    key_segment = jnp.zeros((ROWS, ROWS), jnp.int32)
    end = 0
    for doc in range(4):
        end = end + lengths[seq, doc]
        query_segment = query_segment + (queries >= end).astype(jnp.int32)
        key_segment = key_segment + (keys >= end).astype(jnp.int32)
    allowed = (query_segment == key_segment) & (keys <= queries)
    return jnp.where(allowed, 0.0, -1e30), (queries - keys).astype(F32)


def halves_of_pair():
    lanes = lax.broadcasted_iota(jnp.int32, (1, 128), 1).astype(F32)
    low = jnp.where(lanes < HEAD_DIM, 1.0, 0.0).astype(BF)
    high = jnp.where(lanes < HEAD_DIM, 0.0, 1.0).astype(BF)
    return low, high


def main_kernel(
    x_ref, lengths, cot_ref, n1g, n1s, wqkv, qkvb, wdense, denseb, n2g, n2s, wup, upb, wdown, downb,
    y_out, gx_out, dn1g, dn1s, dqkv, dqkvb, ddense, ddenseb, dn2g, dn2s, dup, dupb, ddown, ddownb,
    w, g, sb, r1, r2, r3, q, small, small_in,
    xs, inbox, outbox, a_all, qkv, o_all, p_all, hidden, xh1, xh2, inv1, inv2, c_all, act, slope_u,
    gz_all, gu, gat_all, go, gqkv, part_out, part_in, wide, ghid, send_sems, recv_sems,
):
    place = Place()
    links = Links(send_sems, recv_sems)
    t, other = place.tensor, 1 - place.tensor
    streams = range(SEQS)

    def at_section(number, *steps):
        @pl.when(place.section == number)
        def _():
            for step in steps:
                step()

    barrier = pltpu.get_barrier_semaphore()
    neighbours = [
        place.along("y", 1),
        place.along("y", -1),
        place.along("z", 1),
        place.along("z", -1),
        place.sibling(),
        place.peer(),
        place.other_section(),
    ]
    for neighbour in neighbours:
        pl.semaphore_signal(barrier, inc=1, device_id=neighbour, device_id_type=MESH)
    for half in range(2):
        rows = slice(half * 16, half * 16 + 16)
        here = w.at[place.z, place.y, place.core, half]
        for kind in range(3):
            here[:, kind * WIDTH : (kind + 1) * WIDTH] = wqkv[0, kind, rows, :]
        for ref, start in ((wdense, DENSE_AT), (wup, UP_AT), (wdown, DOWN_AT)):
            here[:, start : start + ref.shape[2]] = ref[0, rows, :]
    pl.semaphore_wait(barrier, len(neighbours))

    def share(name, ref, s):
        links.send((name, s), lambda: ref.at[s, t], ref.at[s, t], place.peer())

    def shared(name, ref, s):
        links.arrived((name, s), ref.at[s, other], place.peer())

    def partial(name, k, s, start, count, source):
        rows = jnp.concatenate([source[s, other], source[s, t]], axis=0)

        for i in range(4):
            cols = pl.ds(i * 256, 256)
            value = mm(rows, w[i, :, :, :, :, start : start + count].reshape(256, count), NT)
            part_out[k, s, :, cols] = value[:HALF].astype(BF)
            wide[k % 2, s, :, cols] = value[HALF:]
        links.send((name, s), lambda: part_out.at[k, s], part_in.at[k, s], place.peer())

    def summed(name, k, s):
        links.arrived((name, s), part_in.at[k, s], place.peer())
        return wide[k % 2, s] + part_in[k, s].astype(F32)

    gather = [gather_steps(place, links, w, number) for number in range(3)]

    def all_gathers():
        for step in range(9):
            for number in range(3):
                gather[number][step]()

    def cotangent_shared():
        for s in streams:
            gz_all[s, t] = cot_ref[s]
            share("gz", gz_all, s)

    qd, up, down = gather
    gain1, shift1 = n1g[...].astype(F32), n1s[...].astype(F32)
    gain2, shift2 = n2g[...].astype(F32), n2s[...].astype(F32)
    masks = halves_of_pair()
    tensor_scale = jnp.where(t == 0, 1.0, 2.0 ** (-8.0 * HEADS_HERE / HEADS))

    def enter(s):
        normed, inverse = normalise(xs[s].astype(F32))
        xh1[s] = normed
        inv1[s] = jnp.broadcast_to(inverse, (HALF, 128))
        a_all[s, t] = (normed * gain1 + shift1).astype(BF)
        share("a", a_all, s)

    def enter_first(s):
        xs[s] = x_ref[s]
        enter(s)

    def enter_second(s):
        links.arrived(("forward", s), inbox.at[s], place.other_section())
        xs[s] = inbox[s]
        enter(s)

    def project(s):
        shared("a", a_all, s)
        rows = a_all[s].reshape(ROWS, D)
        for kind in range(3):
            cols = slice(kind * WIDTH, (kind + 1) * WIDTH)
            value = mm(rows, whole_columns(w, cols)) + qkvb[0, kind : kind + 1].astype(F32)
            qkv[s, :, :, cols] = value.astype(BF).reshape(2, HALF, WIDTH)

    def heads_of(ref, s, kind, pair):
        at = kind * WIDTH + pair * 128
        return ref[s, :, :, at : at + 128].reshape(ROWS, 128)

    def attend(s):
        bias, distance = score_bias(lengths, s)
        distance = distance * tensor_scale
        for pair in range(HEADS_HERE // 2):
            queries, keys, values = (heads_of(qkv, s, kind, pair) for kind in range(3))
            mixed = None
            for side in range(2):
                head = pair * 2 + side
                slope = 2.0 ** (-8.0 * (head + 1) / HEADS)
                scores = mm(queries * masks[side], keys, NT) * HEAD_DIM ** (-0.5)
                scores = scores + (bias - slope * distance)
                exponent = jnp.exp(scores - jnp.max(scores, axis=-1, keepdims=True))
                chances = exponent / jnp.sum(exponent, axis=-1, keepdims=True)
                p_all[s, head] = chances
                term = mm(chances.astype(BF), values * masks[side])
                mixed = term if mixed is None else mixed + term
            cols = slice(pair * 128, pair * 128 + 128)
            o_all[s, :, :, cols] = mixed.astype(BF).reshape(2, HALF, 128)
        partial("attended", 0, s, DENSE_AT, WIDTH, o_all)

    def middle(s):
        value = xs[s].astype(F32) + denseb[...].astype(F32)
        value = value + summed("attended", 0, s)
        hidden[s] = value
        normed, inverse = normalise(value)
        xh2[s] = normed
        inv2[s] = jnp.broadcast_to(inverse, (HALF, 128))
        c_all[s, t] = (normed * gain2 + shift2).astype(BF)
        share("c", c_all, s)

    def expand(s):
        shared("c", c_all, s)
        rows = c_all[s].reshape(ROWS, D)

        for at in range(0, HIDDEN, TILE):
            u = mm(rows, whole_columns(w, pl.ds(UP_AT + at, TILE)))
            u = u + upb[:, pl.ds(at, TILE)].astype(F32)
            square = u * u
            tanh = jnp.tanh(GELU_A * u * (1.0 + GELU_B * square))
            inner = GELU_A * (1.0 + (3.0 * GELU_B) * square)
            value = (0.5 * u * (1.0 + tanh)).astype(BF)
            act[s, :, :, pl.ds(at, TILE)] = value.reshape(2, HALF, TILE)
            slope = 0.5 * (1.0 + tanh) + 0.5 * u * (1.0 - tanh * tanh) * inner
            slope_u[s, :, :, pl.ds(at, TILE)] = slope.reshape(2, HALF, TILE)

    def contract(s):
        partial("lowered", 1, s, DOWN_AT, HIDDEN, act)

    def leave(s):
        value = hidden[s] + downb[...].astype(F32) + summed("lowered", 1, s)
        outbox[0, s] = value.astype(BF)
        y_out[0, s] = value.astype(BF)

    def forward_copy(s):
        return links.copy(("forward", s), outbox.at[0, s], inbox.at[s], place.other_section())

    def backward_copy(s):
        return links.copy(("backward", s), outbox.at[1, s], inbox.at[s], place.other_section())

    at_section(
        0,
        *(qd[0], up[0], lambda: enter_first(0), lambda: enter_first(1)),
        *(qd[1], qd[2], qd[3], up[1], qd[4], qd[5], up[2], down[0], qd[6]),
        *(qd[7], up[3], down[1], qd[8]),
    )
    at_section(
        1, all_gathers, cotangent_shared, lambda: enter_second(0), lambda: enter_second(1)
    )
    at_section(0, up[4], down[2])
    project(0)
    at_section(0, up[5], down[3])
    attend(0)
    at_section(0, up[6], up[7], down[4])
    project(1)
    at_section(0, down[5])
    attend(1)
    at_section(0, up[8], down[6], down[7])
    middle(0)
    middle(1)
    at_section(0, lambda: expand(0), down[8], lambda: contract(0))
    at_section(0, lambda: expand(1), lambda: contract(1))

    @pl.when(place.section == 0)
    def _():
        for s in streams:
            leave(s)
            forward_copy(s).start()

    @pl.when(place.section == 0)
    def _():
        for s in streams:
            links.arrived(("backward", s), inbox.at[s], place.other_section())
            gz_all[s, t] = inbox[s]
            share("gz", gz_all, s)

    sums = [0.0] * 6

    def contract_back(s):
        shared("gz", gz_all, s)
        rows = gz_all[s].reshape(ROWS, D)

        for at in range(0, HIDDEN, TILE):
            value = mm(rows, whole_columns(w, pl.ds(DOWN_AT + at, TILE)))
            value = value * slope_u[s, :, :, pl.ds(at, TILE)].reshape(ROWS, TILE)
            gu[s, :, :, pl.ds(at, TILE)] = value.astype(BF).reshape(2, HALF, TILE)
        partial("gc", 2, s, UP_AT, HIDDEN, gu)

    def middle_back(s):
        grad = summed("gc", 2, s)
        normed = xh2[s]
        gy = gz_all[s, t].astype(F32)
        sums[3] = sums[3] + column_sum(grad * normed)
        sums[4] = sums[4] + column_sum(grad)
        sums[5] = sums[5] + column_sum(gy)
        value = gy + normalise_back(grad, normed, inv2[s][:, 0:1], gain2)
        ghid[s] = value
        sums[2] = sums[2] + column_sum(value)
        gat_all[s, t] = value.astype(BF)
        share("gat", gat_all, s)

    def attend_back(s):
        if s == 0:
            shared("gat", gat_all, s)
        rows = gat_all[s].reshape(ROWS, D)
        value = mm(rows, whole_columns(w, slice(DENSE_AT, DENSE_AT + WIDTH)))
        go[s] = value.astype(BF).reshape(2, HALF, WIDTH)
        for pair in range(HEADS_HERE // 2):
            queries, keys, values = (heads_of(qkv, s, kind, pair) for kind in range(3))
            grads = heads_of(go, s, 0, pair)
            totals = [None, None, None]
            for side in range(2):
                chances = p_all[s, pair * 2 + side]
                out_grad = grads * masks[side]
                chance_grad = mm(out_grad, values, NT)
                inner = jnp.sum(chances * chance_grad, axis=-1, keepdims=True)
                score_grad = (chances * (chance_grad - inner)).astype(BF)
                terms = (
                    mm(score_grad, keys * masks[side]),
                    mm(score_grad, queries * masks[side], TN),
                    mm(chances.astype(BF), out_grad, TN),
                )
                totals = [b if a is None else a + b for a, b in zip(totals, terms)]
            scale = HEAD_DIM ** (-0.5)
            for kind, value in enumerate((totals[0] * scale, totals[1] * scale, totals[2])):
                at = kind * WIDTH + pair * 128
                gqkv[s, :, :, at : at + 128] = value.astype(BF).reshape(2, HALF, 128)
        partial("ga", 4, s, QKV_AT, 3 * WIDTH, gqkv)

    def leave_back(s):
        grad = summed("ga", 4, s)
        normed = xh1[s]
        sums[0] = sums[0] + column_sum(grad * normed)
        sums[1] = sums[1] + column_sum(grad)
        value = ghid[s] + normalise_back(grad, normed, inv1[s][:, 0:1], gain1)
        outbox[1, s] = value.astype(BF)
        gx_out[0, s] = value.astype(BF)

        @pl.when(place.section == 1)
        def _():
            backward_copy(s).start()

    def finish_qkv(rows, value):
        for kind in range(3):
            dqkv[0, kind, rows, :] = value(kind * WIDTH)

    def finish_up(rows, value):
        ddense[0, rows, :] = value(0)
        for at in range(0, HIDDEN, TILE):
            dup[0, rows, at : at + TILE] = value(WIDTH + at)

    def finish_down(rows, value):
        for at in range(0, HIDDEN, TILE):
            ddown[0, rows, at : at + TILE] = value(at)

    sc_qkv, sc_up, sc_down = (
        scatter_steps(place, links, g, start, count, sb, r1, r2, r3, q, finish)
        for start, count, finish in (
            (QKV_AT, 3 * WIDTH, finish_qkv),
            (DENSE_AT, WIDTH + HIDDEN, finish_up),
            (DOWN_AT, HIDDEN, finish_down),
        )
    )

    def grad_down():
        weight_grad(g, gz_all, act, DOWN_AT, HIDDEN)

    def grad_up():
        weight_grad(g, c_all, gu, UP_AT, HIDDEN)

    def grad_dense():
        weight_grad(g, gat_all, o_all, DENSE_AT, WIDTH)

    at_section(0, lambda: contract_back(0), lambda: contract_back(1))
    at_section(1, *(lambda s=s: (expand(s), contract_back(s)) for s in streams))
    middle_back(0)
    grad_down()
    at_section(0, sc_down[0])
    middle_back(1)
    at_section(0, grad_up, sc_down[1], sc_down[2])
    attend_back(0)
    at_section(0, lambda: shared("gat", gat_all, 1), grad_dense, sc_up[0])
    at_section(1, lambda: shared("gat", gat_all, 1))
    attend_back(1)
    at_section(0, sc_down[3], sc_down[4], sc_up[1], sc_up[2])
    leave_back(0)
    leave_back(1)
    at_section(1, grad_up, grad_dense)
    weight_grad(g, a_all, gqkv, QKV_AT, 3 * WIDTH)
    at_section(0, sc_qkv[0], sc_up[3], sc_up[4], sc_down[5])

    small[0, 6:8] = jnp.zeros((2, D), F32)
    small[0, 12:16] = jnp.zeros((4, D), F32)
    for row in range(6):
        small[0, row : row + 1] = sums[row]
    for i in range(2):
        piece = gu[:, :, :, i * D : (i + 1) * D].reshape(SEQS * ROWS, D).astype(F32)
        small[0, 8 + i : 9 + i] = column_sum(piece)
    piece = gqkv[:, :, :, 0:D].reshape(SEQS * ROWS, D).astype(F32)
    small[0, 10:11] = column_sum(piece)
    piece = gqkv[:, :, :, D : 3 * WIDTH].reshape(SEQS * ROWS, WIDTH).astype(F32)
    small[0, 11:12, 0:WIDTH] = column_sum(piece)
    small[0, 11:12, WIDTH:D] = jnp.zeros((1, D - WIDTH), F32)

    tiny = small_steps(place, links, small, small_in)
    at_section(
        0,
        *(tiny[0], sc_qkv[1], sc_qkv[2], tiny[1], sc_up[5], sc_down[6], tiny[2], sc_qkv[3]),
        *(tiny[3], sc_qkv[4], sc_down[7], sc_up[6], tiny[4], sc_qkv[5], sc_up[7], tiny[5]),
        *(sc_qkv[6], tiny[6], sc_qkv[7]),
    )
    last = [sc_down[0], sc_up[0], sc_qkv[0], lambda: contract(0), lambda: contract(1)]
    for step in range(1, 8):
        last += [tiny[step - 1], sc_down[step], sc_up[step], sc_qkv[step]]
    last += [lambda: leave(0), lambda: leave(1)]
    at_section(1, *last)

    for row, out in enumerate((dn1g, dn1s, ddenseb, dn2g, dn2s, ddownb)):
        out[...] = small[6, row : row + 1]
    dupb[:, 0:D] = small[6, 8:9]
    dupb[:, D : 2 * D] = small[6, 9:10]
    dqkvb[0] = small[6, 10:11, 0:WIDTH]
    dqkvb[1] = small[6, 10:11, WIDTH : 2 * WIDTH]
    dqkvb[2] = small[6, 11:12, 0:WIDTH]

    links.drain(place.sibling())
    at_section(0, *(forward_copy(s).wait_send for s in streams))
    at_section(1, *(backward_copy(s).wait_send for s in streams))


def publish_kernel(*refs):
    count = len(refs) // 2
    sems = refs[-1]
    copies = [pltpu.make_async_copy(refs[i], refs[count + i], sems.at[i]) for i in range(count)]
    for copy in copies:
        copy.start()
    for copy in copies:
        copy.wait()


def local(
    layer_input,
    lengths,
    cotangent,
    norm1_gain,
    norm1_shift,
    qkv_weight,
    qkv_bias,
    dense_weight,
    dense_bias,
    norm2_gain,
    norm2_shift,
    up_weight,
    up_bias,
    down_weight,
    down_bias,
):
    share = qkv_weight.shape[1]
    vmem = pl.BlockSpec(memory_space=pltpu.VMEM)
    smem = pl.BlockSpec(memory_space=pltpu.SMEM)
    shape = jax.ShapeDtypeStruct
    tokens = (SEQS, HALF, D)
    tokens_out = shape((1,) + tokens, BF)
    row = shape((1, D), F32)
    out_shape = (
        tokens_out,
        tokens_out,
        row,
        row,
        shape((1, 3, share, WIDTH), F32),
        shape((3, 1, WIDTH), F32),
        shape((1, share, WIDTH), F32),
        row,
        row,
        row,
        shape((1, share, HIDDEN), F32),
        shape((1, HIDDEN), F32),
        shape((1, share, HIDDEN), F32),
        row,
    )
    block = (4, 4, 2, 2, 16, COLUMNS)

    def all_tokens(width, dtype):
        return pltpu.VMEM((SEQS, 2, HALF, width), dtype)

    scratch = [
        pltpu.VMEM(block, BF),
        pltpu.VMEM(block, BF),
        pltpu.VMEM((2, 4, 4, 16, COLUMNS), BF),
        pltpu.VMEM((2, 4, 16, COLUMNS), BF),
        pltpu.VMEM((2, 4, 16, COLUMNS), BF),
        pltpu.VMEM((2, 4, 16, COLUMNS), BF),
        pltpu.VMEM((2, 3, 16, COLUMNS), BF),
        pltpu.VMEM((7, 16, D), F32),
        pltpu.VMEM((6, 16, D), F32),
        pltpu.VMEM(tokens, BF),
        pltpu.VMEM(tokens, BF),
        pltpu.VMEM((2,) + tokens, BF),
        all_tokens(D, BF),
        all_tokens(3 * WIDTH, BF),
        all_tokens(WIDTH, BF),
        pltpu.VMEM((SEQS, HEADS_HERE, ROWS, ROWS), F32),
        pltpu.VMEM(tokens, F32),
        pltpu.VMEM(tokens, F32),
        pltpu.VMEM(tokens, F32),
        pltpu.VMEM((SEQS, HALF, 128), F32),
        pltpu.VMEM((SEQS, HALF, 128), F32),
        all_tokens(D, BF),
        all_tokens(HIDDEN, BF),
        all_tokens(HIDDEN, F32),
        all_tokens(D, BF),
        all_tokens(HIDDEN, BF),
        all_tokens(D, BF),
        all_tokens(WIDTH, BF),
        all_tokens(3 * WIDTH, BF),
        pltpu.VMEM((5,) + tokens, BF),
        pltpu.VMEM((5,) + tokens, BF),
        pltpu.VMEM((2,) + tokens, F32),
        pltpu.VMEM(tokens, F32),
        pltpu.SemaphoreType.DMA((208,)),
        pltpu.SemaphoreType.DMA((208,)),
    ]
    outs = pl.pallas_call(
        main_kernel,
        out_shape=out_shape,
        in_specs=[vmem, smem] + [vmem] * 13,
        out_specs=[vmem] * 14,
        scratch_shapes=scratch,
        compiler_params=pltpu.CompilerParams(
            collective_id=0, has_side_effects=True, vmem_limit_bytes=63 * 2**20
        ),
    )(
        layer_input,
        lengths,
        cotangent,
        norm1_gain,
        norm1_shift,
        jnp.transpose(qkv_weight, (0, 2, 1, 3)),
        qkv_bias,
        dense_weight,
        dense_bias,
        norm2_gain,
        norm2_shift,
        up_weight,
        up_bias,
        down_weight,
        down_bias,
    )
    outs = pl.pallas_call(
        publish_kernel,
        out_shape=out_shape,
        in_specs=[pl.BlockSpec(memory_space=pl.ANY)] * 14,
        out_specs=[vmem] * 14,
        scratch_shapes=[pltpu.SemaphoreType.DMA((14,))],
        compiler_params=pltpu.CompilerParams(vmem_limit_bytes=62 * 2**20),
    )(*outs)
    outs = list(outs)
    outs[4] = jnp.transpose(outs[4], (0, 2, 1, 3))
    outs[5] = jnp.transpose(outs[5], (1, 0, 2))
    return tuple(outs)


def solution(mesh):
    in_specs = (
        P("dp", "tensor", None),
        P("dp", None),
        P("dp", "tensor", None),
        P("section", None),
        P("section", None),
        P("section", "dp", None, "tensor"),
        P("section", None, "tensor"),
        P("section", "dp", "tensor"),
        P("section", None),
        P("section", None),
        P("section", None),
        P("section", "dp", "tensor"),
        P("section", "tensor"),
        P("section", "dp", "tensor"),
        P("section", None),
    )
    out_specs = (
        P("section", "dp", "tensor", None),
        P("section", "dp", "tensor", None),
        P("section", None),
        P("section", None),
        P("section", "dp", None, "tensor"),
        P("section", None, "tensor"),
        P("section", "dp", "tensor"),
        P("section", None),
        P("section", None),
        P("section", None),
        P("section", "dp", "tensor"),
        P("section", "tensor"),
        P("section", "dp", "tensor"),
        P("section", None),
    )
    return jax.shard_map(local, mesh=mesh, in_specs=in_specs, out_specs=out_specs, check_vma=False)
```

```python
import jax
import jax.numpy as jnp
from jax import lax
from jax.experimental import pallas as pl
from jax.experimental.pallas import tpu as pltpu
from jax.sharding import PartitionSpec as P

D = 1024
HEADS = 16
HEAD_DIM = 64
FF = 4096
ROWS = 128
EPSILON = 1e-05
GELU_A = 0.79788456
GELU_B = 0.044715

SEQS = 2
HALF = 64
HEADS_HERE = HEADS // 2
WIDTH = HEADS_HERE * HEAD_DIM
HIDDEN = FF // 2
QKV_AT = 0
DENSE_AT = 3 * WIDTH
UP_AT = DENSE_AT + WIDTH
DOWN_AT = UP_AT + HIDDEN
COLUMNS = DOWN_AT + HIDDEN
TILE = 512
GROUP = 2048
GROUP_QD, GROUP_UP, GROUP_DOWN = 0, 1, 2

BF = jnp.bfloat16
F32 = jnp.float32
MESH = pl.DeviceIdType.MESH

NN = (((1,), (0,)), ((), ()))
NT = (((1,), (1,)), ((), ()))
TN = (((0,), (0,)), ((), ()))


def mm(left, right, dims=NN):
    return lax.dot_general(left, right, dims, preferred_element_type=F32)


class Links:
    def __init__(self, send_sems, recv_sems):
        self.send_sems = send_sems
        self.recv_sems = recv_sems
        self.names = {}
        self.sources = {}

    def index(self, name):
        return self.names.setdefault(name, len(self.names))

    def copy(self, name, src, dst, device):
        i = self.index(name)
        return pltpu.make_async_remote_copy(
            src_ref=src,
            dst_ref=dst,
            send_sem=self.send_sems.at[i],
            recv_sem=self.recv_sems.at[i],
            device_id=device,
            device_id_type=MESH,
        )

    def send(self, name, source, dst, device):
        self.copy(name, source(), dst, device).start()
        self.sources.setdefault(name, source)

    def arrived(self, name, landing, device):
        self.copy(name, landing, landing, device).wait_recv()

    def drain(self, device):
        for name, source in self.sources.items():
            ref = source()
            self.copy(name, ref, ref, device).wait_send()
        self.sources = {}


def four(value):
    return lax.rem(value + 8, 4)


class Place:
    def __init__(self):
        self.section = lax.axis_index("section")
        self.tensor = lax.axis_index("tensor")
        dp = lax.axis_index("dp")
        self.core = lax.rem(dp, 2)
        self.y = lax.rem(lax.div(dp, 2), 4)
        self.z = lax.div(dp, 8)
        self.d = 1 - 2 * self.core
        self.back = -self.d

    def dp(self, z, y, core):
        return {"dp": (z * 4 + y) * 2 + core}

    def along(self, axis, offset):
        if axis == "y":
            return self.dp(self.z, four(self.y + offset), self.core)
        return self.dp(four(self.z + offset), self.y, self.core)

    def sibling(self):
        return self.dp(self.z, self.y, 1 - self.core)

    def peer(self):
        return {"tensor": 1 - self.tensor}

    def other_section(self):
        return {"section": 1 - self.section}


FIRST = ("y", "z")
SECOND = ("z", "y")


def gather_steps(place, links, w, number):
    z, y, core, d, back = place.z, place.y, place.core, place.d, place.back
    cols = pl.ds(number * GROUP, GROUP)
    firsts = (0, back, d, 2)
    halves = range(2)

    def piece(half, first, second):
        if half == 0:
            return w.at[four(z + second), four(y + first), core, 0, :, cols]
        return w.at[four(z + first), four(y + second), core, 1, :, cols]

    def name_of(name, half):
        return ("gather", number, name, half)

    def send(name, half, spot, axis, offset):
        links.send(
            name_of(name, half),
            lambda: piece(half, *spot),
            piece(half, *spot),
            place.along(axis, offset),
        )

    def arrived(name, half, spot):
        links.arrived(name_of(name, half), piece(half, *spot), place.sibling())

    def second_sends(half, k):
        send(("s+", k), half, (firsts[k], 0), SECOND[half], d)
        send(("s-", k), half, (firsts[k], 0), SECOND[half], back)

    def relay(half, k):
        arrived(("s+", k), half, (firsts[k], back))
        send(("sr", k), half, (firsts[k], back), SECOND[half], d)

    def group(half, second, of_core):
        if half == 0:
            return w.at[four(z + second), :, of_core, 0, :, cols]
        return w.at[:, four(y + second), of_core, 1, :, cols]

    def to_sibling(j, second):
        for half in halves:
            links.send(
                name_of(("swap", j), half),
                lambda half=half: group(half, second, core),
                group(half, second, core),
                place.sibling(),
            )

    def step0():
        for half in halves:
            send("f+", half, (0, 0), FIRST[half], d)
            send("f-", half, (0, 0), FIRST[half], back)
        for half in halves:
            second_sends(half, 0)

    def step1():
        for half in halves:
            arrived("f+", half, (back, 0))
            send("fr", half, (back, 0), FIRST[half], d)
            second_sends(half, 1)

    def step2():
        for half in halves:
            arrived("f-", half, (d, 0))
            second_sends(half, 2)
        for half in halves:
            relay(half, 0)

    def step3():
        for half in halves:
            arrived("fr", half, (2, 0))
            second_sends(half, 3)
        to_sibling(0, 0)

    def step4():
        for k in (1, 2):
            for half in halves:
                relay(half, k)

    def step5():
        for half in halves:
            relay(half, 3)
        to_sibling(1, back)

    def step6():
        for k in range(4):
            for half in halves:
                arrived(("s-", k), half, (firsts[k], d))
        to_sibling(2, d)

    def step7():
        for k in range(4):
            for half in halves:
                arrived(("sr", k), half, (firsts[k], 2))
        to_sibling(3, 2)

    def step8():
        for j, second in enumerate((0, d, back, 2)):
            for half in halves:
                links.arrived(
                    name_of(("swap", j), half), group(half, second, 1 - core), place.sibling()
                )

    return (step0, step1, step2, step3, step4, step5, step6, step7, step8)


def scatter_steps(place, links, g, start, count, sb, r1, r2, r3, q, finish):
    z, y, core, d, back = place.z, place.y, place.core, place.d, place.back
    all_cols = pl.ds(start, count)
    axes, other_axes = ("z", "y"), ("y", "z")
    spots = (y, z)
    mine, theirs = (0, d, back, 2), (0, back, d, 2)
    halves = range(2)

    def name_of(name, half):
        return ("scatter", start, name, half)

    def group(half, offset, of_core):
        if half == 0:
            return g.at[four(z + offset), :, of_core, 0, :, all_cols]
        return g.at[:, four(y + offset), of_core, 1, :, all_cols]

    def own(half, offset, j):
        if half == 0:
            return g[four(z + offset), j, core, 0, :, all_cols].astype(F32)
        return g[j, four(y + offset), core, 1, :, all_cols].astype(F32)

    def add(half, slot, with_own, *others):
        for j in range(4):
            total = sb[half, slot, j, :, all_cols].astype(F32)
            if with_own:
                total = total + own(half, mine[slot], j)
            for other in others:
                total = total + other[half, j, :, all_cols].astype(F32)
            sb[half, slot, j, :, all_cols] = total.astype(BF)

    def swapped(half, slot):
        links.arrived(name_of(("swap", slot), half), sb.at[half, slot, :, :, all_cols], place.sibling())

    def landed(name, half, ref):
        links.arrived(name_of(name, half), ref, place.sibling())

    def step0():
        for slot in (3, 2, 1, 0):
            for half in halves:
                links.send(
                    name_of(("swap", slot), half),
                    lambda slot=slot, half=half: group(half, theirs[slot], 1 - core),
                    sb.at[half, slot, :, :, all_cols],
                    place.sibling(),
                )

    def first_send(name, half, slot, to, offset):
        links.send(
            name_of(name, half),
            lambda: sb.at[half, slot, :, :, all_cols],
            to.at[half, :, :, all_cols],
            place.along(axes[half], offset),
        )

    def step1():
        for half in halves:
            swapped(half, 3)
            add(half, 3, True)
            first_send("r1", half, 3, r1, d)

    def step2():
        for half in halves:
            swapped(half, 2)
            add(half, 2, True)
            first_send("r3", half, 2, r3, back)

    def step3():
        for half in halves:
            swapped(half, 1)
            landed("r1", half, r1.at[half, :, :, all_cols])
            add(half, 1, True, r1)
            first_send("r2", half, 1, r2, d)

    def step4():
        for half in halves:
            swapped(half, 0)
            landed("r3", half, r3.at[half, :, :, all_cols])
            add(half, 0, True, r3)

    def second_send(name, half, src, to, offset):
        links.send(name_of(name, half), src, to, place.along(other_axes[half], offset))

    def step5():
        for half in halves:
            landed("r2", half, r2.at[half, :, :, all_cols])
            add(half, 0, False, r2)
            for name, way, slot, offset in (("q0", 2, 0, d), ("q2", back, 2, back)):
                second_send(
                    name,
                    half,
                    lambda half=half, way=way: sb.at[half, 0, four(spots[half] + way), :, all_cols],
                    q.at[half, slot, :, all_cols],
                    offset,
                )

    def step6():
        for half in halves:
            landed("q0", half, q.at[half, 0, :, all_cols])
            total = q[half, 0, :, all_cols].astype(F32)
            total = total + sb[half, 0, four(spots[half] + d), :, all_cols].astype(F32)
            q[half, 0, :, all_cols] = total.astype(BF)
            second_send(
                "q1", half, lambda half=half: q.at[half, 0, :, all_cols], q.at[half, 1, :, all_cols], d
            )

    def step7():
        for half in halves:
            landed("q2", half, q.at[half, 2, :, all_cols])
            landed("q1", half, q.at[half, 1, :, all_cols])

            def value(at):
                cols = pl.ds(start + at, TILE)
                return (
                    sb[half, 0, spots[half], :, cols].astype(F32)
                    + q[half, 1, :, cols].astype(F32)
                    + q[half, 2, :, cols].astype(F32)
                )

            finish(slice(half * 16, half * 16 + 16), value)

    return (step0, step1, step2, step3, step4, step5, step6, step7)


def small_steps(place, links, small, small_in):
    z, y, core = place.z, place.y, place.core
    partners = (
        place.peer(),
        place.sibling(),
        place.dp(z, y + 1 - 2 * lax.rem(y, 2), core),
        place.dp(z, 3 - y, core),
        place.dp(z + 1 - 2 * lax.rem(z, 2), y, core),
        place.dp(3 - z, y, core),
    )

    def rows_of(step):
        return pl.ds(0, 8 if step == 0 else 16)

    def begin(step):
        rows = rows_of(step)
        links.send(
            ("small", step),
            lambda: small.at[step, rows],
            small_in.at[step, rows],
            partners[step],
        )

    def end(step):
        links.arrived(("small", step), small_in.at[step, rows_of(step)], partners[step])
        if step == 0:
            small[1, 0:8] = small[0, 0:8] + small_in[0, 0:8]
            small[1, 8:16] = small[0, 8:16]
        else:
            small[step + 1] = small[step] + small_in[step]

    def at(step):
        def run():
            if step > 0:
                end(step - 1)
            if step < 6:
                begin(step)

        return run

    return tuple(at(step) for step in range(7))


def normalise(values):
    mean = jnp.mean(values, axis=-1, keepdims=True)
    centred = values - mean
    inverse = lax.rsqrt(jnp.mean(centred * centred, axis=-1, keepdims=True) + EPSILON)
    return centred * inverse, inverse


def normalise_back(grad, normed, inverse, gain):
    scaled = grad * gain
    one = jnp.mean(scaled, axis=-1, keepdims=True)
    two = jnp.mean(scaled * normed, axis=-1, keepdims=True)
    return inverse * (scaled - one - normed * two)


def column_sum(values):
    return jnp.sum(values, axis=0, keepdims=True)


def whole_columns(w, cols):
    return w[:, :, :, :, :, cols].reshape(D, -1)


def weight_grad(g, left, right, start, count):
    for i in range(4):
        piece = left[:, :, :, i * 256 : (i + 1) * 256].reshape(SEQS * ROWS, 256)
        for col in range(0, count, TILE):
            part = right[:, :, :, col : col + TILE].reshape(SEQS * ROWS, TILE)
            value = mm(piece, part, TN).astype(BF)
            g[i, :, :, :, :, start + col : start + col + TILE] = value.reshape(4, 2, 2, 16, TILE)


def score_bias(lengths, seq):
    queries = lax.broadcasted_iota(jnp.int32, (ROWS, ROWS), 0)
    keys = lax.broadcasted_iota(jnp.int32, (ROWS, ROWS), 1)
    query_segment = jnp.zeros((ROWS, ROWS), jnp.int32)
    key_segment = jnp.zeros((ROWS, ROWS), jnp.int32)
    end = 0
    for doc in range(4):
        end = end + lengths[seq, doc]
        query_segment = query_segment + (queries >= end).astype(jnp.int32)
        key_segment = key_segment + (keys >= end).astype(jnp.int32)
    allowed = (query_segment == key_segment) & (keys <= queries)
    return jnp.where(allowed, 0.0, -1e30), (queries - keys).astype(F32)


def halves_of_pair():
    lanes = lax.broadcasted_iota(jnp.int32, (1, 128), 1).astype(F32)
    low = jnp.where(lanes < HEAD_DIM, 1.0, 0.0).astype(BF)
    high = jnp.where(lanes < HEAD_DIM, 0.0, 1.0).astype(BF)
    return low, high


def main_kernel(
    x_in, lengths, cot_in, n1g_in, n1s_in, wqkv, qkvb_in, wdense, denseb_in, n2g_in, n2s_in, wup,
    upb_in, wdown, downb_in,
    y_out, gx_out, dn1g, dn1s, dqkv, dqkvb, ddense, ddenseb, dn2g, dn2s, dup, dupb, ddown, ddownb,
    w, g, sb, r1, r2, r3, q, small, small_in,
    xs, inbox, outbox, a_all, qkv, o_all, p_all, hidden, xh1, xh2, inv1, inv2, c_all, act, slope_u,
    gz_all, gu, gat_all, go, gqkv, part_out, part_in, wide, ghid, send_sems, recv_sems,
    x_ref, cot_ref, n1g, n1s, qkvb, denseb, n2g, n2s, upb, downb, load_sems,
):
    place = Place()
    links = Links(send_sems, recv_sems)
    t, other = place.tensor, 1 - place.tensor
    streams = range(SEQS)

    def at_section(number, *steps):
        @pl.when(place.section == number)
        def _():
            for step in steps:
                step()

    shards, others = [], []
    for half in range(2):
        rows = pl.ds(half * 16, 16)
        here = w.at[place.z, place.y, place.core, half]
        for kind in range(3):
            shards.append((wqkv.at[0, kind, rows], here.at[:, pl.ds(kind * WIDTH, WIDTH)]))
        for ref, start in ((wdense, DENSE_AT), (wup, UP_AT), (wdown, DOWN_AT)):
            shards.append((ref.at[0, rows], here.at[:, pl.ds(start, ref.shape[2])]))
    others += [(x_in, x_ref), (cot_in, cot_ref), (n1g_in, n1g), (n1s_in, n1s), (qkvb_in, qkvb)]
    others += [(denseb_in, denseb), (n2g_in, n2g), (n2s_in, n2s), (upb_in, upb), (downb_in, downb)]
    loads = [
        pltpu.make_async_copy(source, target, load_sems.at[i])
        for i, (source, target) in enumerate(shards + others)
    ]
    for load in loads:
        load.start()

    barrier = pltpu.get_barrier_semaphore()
    neighbours = [
        place.along("y", 1),
        place.along("y", -1),
        place.along("z", 1),
        place.along("z", -1),
        place.sibling(),
        place.peer(),
        place.other_section(),
    ]
    for neighbour in neighbours:
        pl.semaphore_signal(barrier, inc=1, device_id=neighbour, device_id_type=MESH)
    for load in loads[: len(shards)]:
        load.wait()
    pl.semaphore_wait(barrier, len(neighbours))

    def share(name, ref, s):
        links.send((name, s), lambda: ref.at[s, t], ref.at[s, t], place.peer())

    def shared(name, ref, s):
        links.arrived((name, s), ref.at[s, other], place.peer())

    def partial(name, k, s, start, count, source):
        rows = jnp.concatenate([source[s, other], source[s, t]], axis=0)

        for i in range(4):
            cols = pl.ds(i * 256, 256)
            value = mm(rows, w[i, :, :, :, :, start : start + count].reshape(256, count), NT)
            part_out[k, s, :, cols] = value[:HALF].astype(BF)
            wide[k % 2, s, :, cols] = value[HALF:]
        links.send((name, s), lambda: part_out.at[k, s], part_in.at[k, s], place.peer())

    def summed(name, k, s):
        links.arrived((name, s), part_in.at[k, s], place.peer())
        return wide[k % 2, s] + part_in[k, s].astype(F32)

    gather = [gather_steps(place, links, w, number) for number in range(3)]

    def all_gathers():
        for step in range(9):
            for number in range(3):
                gather[number][step]()

    def cotangent_shared():
        for s in streams:
            gz_all[s, t] = cot_ref[s]
            share("gz", gz_all, s)

    qd, up, down = gather
    at_section(0, qd[0], up[0])
    for load in loads[len(shards) :]:
        load.wait()
    gain1, shift1 = n1g[...].astype(F32), n1s[...].astype(F32)
    gain2, shift2 = n2g[...].astype(F32), n2s[...].astype(F32)
    masks = halves_of_pair()
    tensor_scale = jnp.where(t == 0, 1.0, 2.0 ** (-8.0 * HEADS_HERE / HEADS))

    def enter(s):
        normed, inverse = normalise(xs[s].astype(F32))
        xh1[s] = normed
        inv1[s] = jnp.broadcast_to(inverse, (HALF, 128))
        a_all[s, t] = (normed * gain1 + shift1).astype(BF)
        share("a", a_all, s)

    def enter_first(s):
        xs[s] = x_ref[s]
        enter(s)

    def enter_second(s):
        links.arrived(("forward", s), inbox.at[s], place.other_section())
        xs[s] = inbox[s]
        enter(s)

    def project(s):
        shared("a", a_all, s)
        rows = a_all[s].reshape(ROWS, D)
        for kind in range(3):
            cols = slice(kind * WIDTH, (kind + 1) * WIDTH)
            value = mm(rows, whole_columns(w, cols)) + qkvb[0, kind : kind + 1].astype(F32)
            qkv[s, :, :, cols] = value.astype(BF).reshape(2, HALF, WIDTH)

    def heads_of(ref, s, kind, pair):
        at = kind * WIDTH + pair * 128
        return ref[s, :, :, at : at + 128].reshape(ROWS, 128)

    def attend(s):
        bias, distance = score_bias(lengths, s)
        distance = distance * tensor_scale
        for pair in range(HEADS_HERE // 2):
            queries, keys, values = (heads_of(qkv, s, kind, pair) for kind in range(3))
            mixed = None
            for side in range(2):
                head = pair * 2 + side
                slope = 2.0 ** (-8.0 * (head + 1) / HEADS)
                scores = mm(queries * masks[side], keys, NT) * HEAD_DIM ** (-0.5)
                scores = scores + (bias - slope * distance)
                exponent = jnp.exp(scores - jnp.max(scores, axis=-1, keepdims=True))
                chances = exponent / jnp.sum(exponent, axis=-1, keepdims=True)
                p_all[s, head] = chances
                term = mm(chances.astype(BF), values * masks[side])
                mixed = term if mixed is None else mixed + term
            cols = slice(pair * 128, pair * 128 + 128)
            o_all[s, :, :, cols] = mixed.astype(BF).reshape(2, HALF, 128)
        partial("attended", 0, s, DENSE_AT, WIDTH, o_all)

    def middle(s):
        value = xs[s].astype(F32) + denseb[...].astype(F32)
        value = value + summed("attended", 0, s)
        hidden[s] = value
        normed, inverse = normalise(value)
        xh2[s] = normed
        inv2[s] = jnp.broadcast_to(inverse, (HALF, 128))
        c_all[s, t] = (normed * gain2 + shift2).astype(BF)
        share("c", c_all, s)

    def expand(s):
        shared("c", c_all, s)
        rows = c_all[s].reshape(ROWS, D)

        for at in range(0, HIDDEN, TILE):
            u = mm(rows, whole_columns(w, pl.ds(UP_AT + at, TILE)))
            u = u + upb[:, pl.ds(at, TILE)].astype(F32)
            square = u * u
            tanh = jnp.tanh(GELU_A * u * (1.0 + GELU_B * square))
            inner = GELU_A * (1.0 + (3.0 * GELU_B) * square)
            value = (0.5 * u * (1.0 + tanh)).astype(BF)
            act[s, :, :, pl.ds(at, TILE)] = value.reshape(2, HALF, TILE)
            slope = 0.5 * (1.0 + tanh) + 0.5 * u * (1.0 - tanh * tanh) * inner
            slope_u[s, :, :, pl.ds(at, TILE)] = slope.reshape(2, HALF, TILE)

    def contract(s):
        partial("lowered", 1, s, DOWN_AT, HIDDEN, act)

    def leave(s):
        value = hidden[s] + downb[...].astype(F32) + summed("lowered", 1, s)
        outbox[0, s] = value.astype(BF)
        y_out[0, s] = value.astype(BF)

    def forward_copy(s):
        return links.copy(("forward", s), outbox.at[0, s], inbox.at[s], place.other_section())

    def backward_copy(s):
        return links.copy(("backward", s), outbox.at[1, s], inbox.at[s], place.other_section())

    at_section(
        0,
        *(lambda: enter_first(0), lambda: enter_first(1)),
        *(qd[1], qd[2], qd[3], up[1], qd[4], qd[5], up[2], down[0], qd[6]),
        *(qd[7], up[3], down[1], qd[8]),
    )
    at_section(
        1, all_gathers, cotangent_shared, lambda: enter_second(0), lambda: enter_second(1)
    )
    at_section(0, up[4], down[2])
    project(0)
    at_section(0, up[5], down[3])
    attend(0)
    at_section(0, up[6], up[7], down[4])
    project(1)
    at_section(0, down[5])
    attend(1)
    at_section(0, up[8], down[6], down[7])
    middle(0)
    middle(1)
    at_section(0, lambda: expand(0), down[8], lambda: contract(0))
    at_section(0, lambda: expand(1), lambda: contract(1))

    @pl.when(place.section == 0)
    def _():
        for s in streams:
            leave(s)
            forward_copy(s).start()

    @pl.when(place.section == 0)
    def _():
        for s in streams:
            links.arrived(("backward", s), inbox.at[s], place.other_section())
            gz_all[s, t] = inbox[s]
            share("gz", gz_all, s)

    sums = [0.0] * 6

    def contract_back(s):
        shared("gz", gz_all, s)
        rows = gz_all[s].reshape(ROWS, D)

        for at in range(0, HIDDEN, TILE):
            value = mm(rows, whole_columns(w, pl.ds(DOWN_AT + at, TILE)))
            value = value * slope_u[s, :, :, pl.ds(at, TILE)].reshape(ROWS, TILE)
            gu[s, :, :, pl.ds(at, TILE)] = value.astype(BF).reshape(2, HALF, TILE)
        partial("gc", 2, s, UP_AT, HIDDEN, gu)

    def middle_back(s):
        grad = summed("gc", 2, s)
        normed = xh2[s]
        gy = gz_all[s, t].astype(F32)
        sums[3] = sums[3] + column_sum(grad * normed)
        sums[4] = sums[4] + column_sum(grad)
        sums[5] = sums[5] + column_sum(gy)
        value = gy + normalise_back(grad, normed, inv2[s][:, 0:1], gain2)
        ghid[s] = value
        sums[2] = sums[2] + column_sum(value)
        gat_all[s, t] = value.astype(BF)
        share("gat", gat_all, s)

    def attend_back(s):
        if s == 0:
            shared("gat", gat_all, s)
        rows = gat_all[s].reshape(ROWS, D)
        value = mm(rows, whole_columns(w, slice(DENSE_AT, DENSE_AT + WIDTH)))
        go[s] = value.astype(BF).reshape(2, HALF, WIDTH)
        for pair in range(HEADS_HERE // 2):
            queries, keys, values = (heads_of(qkv, s, kind, pair) for kind in range(3))
            grads = heads_of(go, s, 0, pair)
            totals = [None, None, None]
            for side in range(2):
                chances = p_all[s, pair * 2 + side]
                out_grad = grads * masks[side]
                chance_grad = mm(out_grad, values, NT)
                inner = jnp.sum(chances * chance_grad, axis=-1, keepdims=True)
                score_grad = (chances * (chance_grad - inner)).astype(BF)
                terms = (
                    mm(score_grad, keys * masks[side]),
                    mm(score_grad, queries * masks[side], TN),
                    mm(chances.astype(BF), out_grad, TN),
                )
                totals = [b if a is None else a + b for a, b in zip(totals, terms)]
            scale = HEAD_DIM ** (-0.5)
            for kind, value in enumerate((totals[0] * scale, totals[1] * scale, totals[2])):
                at = kind * WIDTH + pair * 128
                gqkv[s, :, :, at : at + 128] = value.astype(BF).reshape(2, HALF, 128)
        partial("ga", 4, s, QKV_AT, 3 * WIDTH, gqkv)

    def leave_back(s):
        grad = summed("ga", 4, s)
        normed = xh1[s]
        sums[0] = sums[0] + column_sum(grad * normed)
        sums[1] = sums[1] + column_sum(grad)
        value = ghid[s] + normalise_back(grad, normed, inv1[s][:, 0:1], gain1)
        outbox[1, s] = value.astype(BF)
        gx_out[0, s] = value.astype(BF)

        @pl.when(place.section == 1)
        def _():
            backward_copy(s).start()

    def finish_qkv(rows, value):
        for kind in range(3):
            dqkv[0, kind, rows, :] = value(kind * WIDTH)

    def finish_up(rows, value):
        ddense[0, rows, :] = value(0)
        for at in range(0, HIDDEN, TILE):
            dup[0, rows, at : at + TILE] = value(WIDTH + at)

    def finish_down(rows, value):
        for at in range(0, HIDDEN, TILE):
            ddown[0, rows, at : at + TILE] = value(at)

    sc_qkv, sc_up, sc_down = (
        scatter_steps(place, links, g, start, count, sb, r1, r2, r3, q, finish)
        for start, count, finish in (
            (QKV_AT, 3 * WIDTH, finish_qkv),
            (DENSE_AT, WIDTH + HIDDEN, finish_up),
            (DOWN_AT, HIDDEN, finish_down),
        )
    )

    def grad_down():
        weight_grad(g, gz_all, act, DOWN_AT, HIDDEN)

    def grad_up():
        weight_grad(g, c_all, gu, UP_AT, HIDDEN)

    def grad_dense():
        weight_grad(g, gat_all, o_all, DENSE_AT, WIDTH)

    at_section(0, lambda: contract_back(0), lambda: contract_back(1))
    at_section(1, *(lambda s=s: (expand(s), contract_back(s)) for s in streams))
    middle_back(0)
    grad_down()
    at_section(0, sc_down[0])
    middle_back(1)
    at_section(0, grad_up, sc_down[1], sc_down[2])
    attend_back(0)
    at_section(0, lambda: shared("gat", gat_all, 1), grad_dense, sc_up[0])
    at_section(1, lambda: shared("gat", gat_all, 1))
    attend_back(1)
    at_section(0, sc_down[3], sc_down[4], sc_up[1], sc_up[2])
    leave_back(0)
    leave_back(1)
    at_section(1, grad_up, grad_dense)
    weight_grad(g, a_all, gqkv, QKV_AT, 3 * WIDTH)
    at_section(0, sc_qkv[0])

    small[0, 6:8] = jnp.zeros((2, D), F32)
    small[0, 12:16] = jnp.zeros((4, D), F32)
    for row in range(6):
        small[0, row : row + 1] = sums[row]
    for i in range(2):
        piece = gu[:, :, :, i * D : (i + 1) * D].reshape(SEQS * ROWS, D).astype(F32)
        small[0, 8 + i : 9 + i] = column_sum(piece)
    piece = gqkv[:, :, :, 0:D].reshape(SEQS * ROWS, D).astype(F32)
    small[0, 10:11] = column_sum(piece)
    piece = gqkv[:, :, :, D : 3 * WIDTH].reshape(SEQS * ROWS, WIDTH).astype(F32)
    small[0, 11:12, 0:WIDTH] = column_sum(piece)
    small[0, 11:12, WIDTH:D] = jnp.zeros((1, D - WIDTH), F32)

    tiny = small_steps(place, links, small, small_in)
    at_section(
        0,
        *(tiny[0], sc_down[5], sc_qkv[1], sc_qkv[2], sc_up[3], sc_up[4], tiny[1], sc_down[6]),
        *(sc_qkv[3], tiny[2], sc_up[5], sc_qkv[4], tiny[3], sc_down[7], sc_up[6], sc_qkv[5]),
        *(tiny[4], sc_up[7], sc_qkv[6], tiny[5], tiny[6], sc_qkv[7]),
    )
    last = [sc_down[0], sc_up[0], sc_qkv[0], lambda: contract(0), lambda: contract(1)]
    for step in range(1, 8):
        last += [tiny[step - 1], sc_down[step], sc_up[step], sc_qkv[step]]
    last += [lambda: leave(0), lambda: leave(1)]
    at_section(1, *last)

    for row, out in enumerate((dn1g, dn1s, ddenseb, dn2g, dn2s, ddownb)):
        out[...] = small[6, row : row + 1]
    dupb[:, 0:D] = small[6, 8:9]
    dupb[:, D : 2 * D] = small[6, 9:10]
    dqkvb[0] = small[6, 10:11, 0:WIDTH]
    dqkvb[1] = small[6, 10:11, WIDTH : 2 * WIDTH]
    dqkvb[2] = small[6, 11:12, 0:WIDTH]

    links.drain(place.sibling())
    at_section(0, *(forward_copy(s).wait_send for s in streams))
    at_section(1, *(backward_copy(s).wait_send for s in streams))


def publish_kernel(*refs):
    count = len(refs) // 2
    sems = refs[-1]
    copies = [pltpu.make_async_copy(refs[i], refs[count + i], sems.at[i]) for i in range(count)]
    for copy in copies:
        copy.start()
    for copy in copies:
        copy.wait()


def local(
    layer_input,
    lengths,
    cotangent,
    norm1_gain,
    norm1_shift,
    qkv_weight,
    qkv_bias,
    dense_weight,
    dense_bias,
    norm2_gain,
    norm2_shift,
    up_weight,
    up_bias,
    down_weight,
    down_bias,
):
    share = qkv_weight.shape[1]
    vmem = pl.BlockSpec(memory_space=pltpu.VMEM)
    anywhere = pl.BlockSpec(memory_space=pl.ANY)
    smem = pl.BlockSpec(memory_space=pltpu.SMEM)
    shape = jax.ShapeDtypeStruct
    tokens = (SEQS, HALF, D)
    tokens_out = shape((1,) + tokens, BF)
    row = shape((1, D), F32)
    out_shape = (
        tokens_out,
        tokens_out,
        row,
        row,
        shape((1, 3, share, WIDTH), F32),
        shape((3, 1, WIDTH), F32),
        shape((1, share, WIDTH), F32),
        row,
        row,
        row,
        shape((1, share, HIDDEN), F32),
        shape((1, HIDDEN), F32),
        shape((1, share, HIDDEN), F32),
        row,
    )
    block = (4, 4, 2, 2, 16, COLUMNS)

    def all_tokens(width, dtype):
        return pltpu.VMEM((SEQS, 2, HALF, width), dtype)

    scratch = [
        pltpu.VMEM(block, BF),
        pltpu.VMEM(block, BF),
        pltpu.VMEM((2, 4, 4, 16, COLUMNS), BF),
        pltpu.VMEM((2, 4, 16, COLUMNS), BF),
        pltpu.VMEM((2, 4, 16, COLUMNS), BF),
        pltpu.VMEM((2, 4, 16, COLUMNS), BF),
        pltpu.VMEM((2, 3, 16, COLUMNS), BF),
        pltpu.VMEM((7, 16, D), F32),
        pltpu.VMEM((6, 16, D), F32),
        pltpu.VMEM(tokens, BF),
        pltpu.VMEM(tokens, BF),
        pltpu.VMEM((2,) + tokens, BF),
        all_tokens(D, BF),
        all_tokens(3 * WIDTH, BF),
        all_tokens(WIDTH, BF),
        pltpu.VMEM((SEQS, HEADS_HERE, ROWS, ROWS), F32),
        pltpu.VMEM(tokens, F32),
        pltpu.VMEM(tokens, F32),
        pltpu.VMEM(tokens, F32),
        pltpu.VMEM((SEQS, HALF, 128), F32),
        pltpu.VMEM((SEQS, HALF, 128), F32),
        all_tokens(D, BF),
        all_tokens(HIDDEN, BF),
        all_tokens(HIDDEN, F32),
        all_tokens(D, BF),
        all_tokens(HIDDEN, BF),
        all_tokens(D, BF),
        all_tokens(WIDTH, BF),
        all_tokens(3 * WIDTH, BF),
        pltpu.VMEM((5,) + tokens, BF),
        pltpu.VMEM((5,) + tokens, BF),
        pltpu.VMEM((2,) + tokens, F32),
        pltpu.VMEM(tokens, F32),
        pltpu.SemaphoreType.DMA((208,)),
        pltpu.SemaphoreType.DMA((208,)),
        pltpu.VMEM(tokens, BF),
        pltpu.VMEM(tokens, BF),
        pltpu.VMEM((1, D), BF),
        pltpu.VMEM((1, D), BF),
        pltpu.VMEM((1, 3, WIDTH), BF),
        pltpu.VMEM((1, D), BF),
        pltpu.VMEM((1, D), BF),
        pltpu.VMEM((1, D), BF),
        pltpu.VMEM((1, HIDDEN), BF),
        pltpu.VMEM((1, D), BF),
        pltpu.SemaphoreType.DMA((24,)),
    ]
    outs = pl.pallas_call(
        main_kernel,
        out_shape=out_shape,
        in_specs=[anywhere, smem] + [anywhere] * 13,
        out_specs=[vmem] * 14,
        scratch_shapes=scratch,
        compiler_params=pltpu.CompilerParams(
            collective_id=0, has_side_effects=True, vmem_limit_bytes=63 * 2**20
        ),
    )(
        layer_input,
        lengths,
        cotangent,
        norm1_gain,
        norm1_shift,
        jnp.transpose(qkv_weight, (0, 2, 1, 3)),
        qkv_bias,
        dense_weight,
        dense_bias,
        norm2_gain,
        norm2_shift,
        up_weight,
        up_bias,
        down_weight,
        down_bias,
    )
    outs = pl.pallas_call(
        publish_kernel,
        out_shape=out_shape,
        in_specs=[anywhere] * 14,
        out_specs=[vmem] * 14,
        scratch_shapes=[pltpu.SemaphoreType.DMA((14,))],
        compiler_params=pltpu.CompilerParams(vmem_limit_bytes=62 * 2**20),
    )(*outs)
    outs = list(outs)
    outs[4] = jnp.transpose(outs[4], (0, 2, 1, 3))
    outs[5] = jnp.transpose(outs[5], (1, 0, 2))
    return tuple(outs)


def solution(mesh):
    in_specs = (
        P("dp", "tensor", None),
        P("dp", None),
        P("dp", "tensor", None),
        P("section", None),
        P("section", None),
        P("section", "dp", None, "tensor"),
        P("section", None, "tensor"),
        P("section", "dp", "tensor"),
        P("section", None),
        P("section", None),
        P("section", None),
        P("section", "dp", "tensor"),
        P("section", "tensor"),
        P("section", "dp", "tensor"),
        P("section", None),
    )
    out_specs = (
        P("section", "dp", "tensor", None),
        P("section", "dp", "tensor", None),
        P("section", None),
        P("section", None),
        P("section", "dp", None, "tensor"),
        P("section", None, "tensor"),
        P("section", "dp", "tensor"),
        P("section", None),
        P("section", None),
        P("section", None),
        P("section", "dp", "tensor"),
        P("section", "tensor"),
        P("section", "dp", "tensor"),
        P("section", None),
    )
    return jax.shard_map(local, mesh=mesh, in_specs=in_specs, out_specs=out_specs, check_vma=False)
```
